256 devices in a mesh: blk: 64 (over y, z, core), hd: 4 (over x).
Axes of the slice: x: 4, y: 4, z: 8, core: 2. Of those that a mesh axis runs over, the one named last changes fastest.
Arguments:
- queries: bfloat16 [1024, 256, 128], P('blk', 'hd'), may hold values from -10 to 10
- keys: bfloat16 [1024, 256, 128], P('blk', 'hd'), may hold values from -10 to 10
- values: bfloat16 [1024, 256, 128], P('blk', 'hd'), may hold values from -6 to 6
- out_weight: bfloat16 [256, 256], P('hd'), may hold values from -0.375 to 0.375
- out_grad: bfloat16 [1024, 128, 256], P('blk'), may hold values from -6 to 6
- pair_list: int32 [2, 2048], replicated, may hold values from 0 to 1023, as said below
Outputs:
- out: bfloat16 [1024, 128, 256], P('blk', 'hd')
- grad_q: bfloat16 [1024, 256, 128], P('blk', 'hd')
- grad_k: bfloat16 [1024, 256, 128], P('blk', 'hd')
- grad_v: bfloat16 [1024, 256, 128], P('blk', 'hd')
The draws below stay inside these ranges and needn't reach their ends.
Inputs may be any that keep to these rules, and one draw needn't show every extreme that they name: `pair_list`: row 0 holds each pair's first block and row 1 its second. Pairs k * 32 to (k + 1) * 32 - 1 have their first block among blocks k * 16 to (k + 1) * 16 - 1; of these pairs at most 2 have their second block in any one range j * 16 to (j + 1) * 16 - 1, and exactly 2 for some range.
All inputs are finite; a program needn't handle non-finite values.
Results may differ from the reference program's by a relative error of at most 0.015.
Values may be sent and summed in bfloat16 or wider, within the bound.
A program may use at most 128 MiB of HBM per device.

```python
import jax
import jax.numpy as jnp
from jax import lax

D = 256
HEAD = 32
BLOCK = 128
BLK_DEV = 16
PAIR_DEV = 32
CAP = 2
BLOCKS = 1024
N_BLK = 64


def draw_queries(key, part):
    key = jax.random.fold_in(key, 1)
    full_shape = (BLOCKS, D, BLOCK)
    result_values = jnp.clip(jax.random.normal(key, full_shape, jnp.float32), -10.0, 10.0)
    return result_values.astype(jnp.bfloat16)


def draw_keys(key, part):
    key = jax.random.fold_in(key, 3)
    full_shape = (BLOCKS, D, BLOCK)
    result_values = jnp.clip(jax.random.normal(key, full_shape, jnp.float32), -10.0, 10.0)
    return result_values.astype(jnp.bfloat16)


def draw_pair_list(key, part):
    key = jax.random.fold_in(key, 11)
    key_first, key_forced, key_others, key_order, key_second = jax.random.split(key, 5)
    slot_total = N_BLK * CAP
    owner_rows = jnp.arange(N_BLK, dtype=jnp.int32)
    first_local = jax.random.randint(key_first, (N_BLK, PAIR_DEV), 0, BLK_DEV, jnp.int32)
    forced_peer = jax.random.randint(key_forced, (N_BLK,), 0, N_BLK, jnp.int32)
    others = jax.vmap(lambda part_key: jax.random.permutation(part_key, slot_total - CAP))(jax.random.split(key_others, N_BLK)).astype(jnp.int32) + CAP
    leading = jnp.broadcast_to(jnp.arange(CAP, dtype=jnp.int32)[None, :], (N_BLK, CAP))
    keyed = jnp.concatenate([leading, others], axis=1)[:, :PAIR_DEV]
    slot_ids = (keyed + forced_peer[:, None] * CAP) % slot_total
    shuffles = jax.vmap(lambda part_key: jax.random.permutation(part_key, PAIR_DEV))(jax.random.split(key_order, N_BLK)).astype(jnp.int32)
    slot_ids = jnp.take_along_axis(slot_ids, shuffles, axis=1)
    peer_owner = slot_ids // CAP
    second_local = jax.random.randint(key_second, (N_BLK, PAIR_DEV), 0, BLK_DEV, jnp.int32)
    first_blocks = first_local + owner_rows[:, None] * BLK_DEV
    second_blocks = second_local + peer_owner * BLK_DEV
    return jnp.stack([first_blocks.reshape(-1), second_blocks.reshape(-1)]).astype(jnp.int32)


def levels(key, dims, cuts, low, top_value):
    def one(dim, shards_of):
        draws = jax.random.uniform(jax.random.fold_in(jax.random.fold_in(key, 6), dim), (shards_of,), jnp.float32, low / len(cuts), top_value / len(cuts))
        return jnp.repeat(jnp.exp(draws), dims[dim] // shards_of).reshape((-1,) + (1,) * (len(dims) - dim - 1))

    gain = one(*cuts[0])
    for cut in cuts[1:]:
        gain = gain * one(*cut)
    return gain


def normal_values(rng, dims, scale, limit, pieces=(), kind=jnp.bfloat16):
    gain = levels(rng, dims, pieces, -0.22, 0.18) if pieces else 1.0
    drawn = jax.random.normal(rng, dims, jnp.float32) * scale * gain
    return jnp.minimum(jnp.maximum(drawn, -limit), limit).astype(kind)


def setup_inputs(seed: int = 0) -> dict:
    arg_keys = jax.random.split(jax.random.key(seed), 7)
    return {
        "queries": draw_queries(jax.random.fold_in(arg_keys[6], 71), 0),
        "keys": draw_keys(jax.random.fold_in(arg_keys[6], 71), 0),
        "values": normal_values(arg_keys[2], (BLOCKS, D, BLOCK), 1.0, 6.0, ((0, 64), (1, 4))),
        "out_weight": normal_values(arg_keys[3], (D, D), D ** -0.5, 0.375, ((0, 4),)),
        "out_grad": normal_values(arg_keys[4], (BLOCKS, BLOCK, D), 1.0, 6.0, ((0, 64),)),
        "pair_list": draw_pair_list(jax.random.fold_in(arg_keys[6], 71), 0),
    }


def lowered(tensor):
    return lax.optimization_barrier(tensor.astype(jnp.bfloat16)).astype(tensor.dtype)


def tile_forward(q_tile, k_tile, v_tile):
    tile_count, feature_count, block_rows = q_tile.shape
    head_count = feature_count // HEAD
    four_shape = (tile_count, head_count, HEAD, block_rows)
    q_four = q_tile.astype(jnp.float32).reshape(four_shape)
    k_four = k_tile.astype(jnp.float32).reshape(four_shape)
    v_four = v_tile.astype(jnp.float32).reshape(four_shape)
    scores = jnp.einsum("nher,nhec->nhrc", q_four, k_four) * (HEAD ** -0.5)
    row_top = jnp.max(scores, axis=3, keepdims=True)
    expo_scores = jnp.exp(scores - row_top)
    row_total = jnp.sum(expo_scores, axis=3, keepdims=True)
    tile_lse = (row_top + jnp.log(row_total))[..., 0]
    weights = (expo_scores / row_total).astype(jnp.bfloat16)
    tile_part = jnp.einsum("nhrc,nhec->nher", weights.astype(jnp.float32), v_four)
    return tile_part.reshape(tile_count, feature_count, block_rows), tile_lse


def tile_backward(q_tile, k_tile, v_tile, grad_tile, lse_tile, delta_tile):
    tile_count, feature_count, block_rows = q_tile.shape
    head_count = feature_count // HEAD
    four_shape = (tile_count, head_count, HEAD, block_rows)
    q_four = q_tile.astype(jnp.float32).reshape(four_shape)
    k_four = k_tile.astype(jnp.float32).reshape(four_shape)
    v_four = v_tile.astype(jnp.float32).reshape(four_shape)
    g_four = grad_tile.astype(jnp.float32).reshape(four_shape)
    score_scale = HEAD ** -0.5
    scores = jnp.einsum("nher,nhec->nhrc", q_four, k_four) * score_scale
    prob = jnp.exp(scores - lse_tile[..., None])
    prob_low = prob.astype(jnp.bfloat16).astype(jnp.float32)
    prob_grad = jnp.einsum("nher,nhec->nhrc", g_four, v_four)
    score_grad = (prob * (prob_grad - delta_tile[..., None])).astype(jnp.bfloat16).astype(jnp.float32)
    term_q = jnp.einsum("nhrc,nhec->nher", score_grad, k_four) * score_scale
    term_k = jnp.einsum("nhrc,nher->nhec", score_grad, q_four) * score_scale
    term_v = jnp.einsum("nhrc,nher->nhec", prob_low, g_four)
    out_shape = (tile_count, feature_count, block_rows)
    return term_q.reshape(out_shape), term_k.reshape(out_shape), term_v.reshape(out_shape)


def reference(queries, keys, values, out_weight, out_grad, pair_list):
    block_count, feature_count, block_rows = queries.shape
    head_count = feature_count // HEAD
    first_blocks = pair_list[0].astype(jnp.int32)
    second_blocks = pair_list[1].astype(jnp.int32)
    pair_count = first_blocks.shape[0]
    own_blocks = jnp.arange(block_count, dtype=jnp.int32)
    query_ids = jnp.concatenate([own_blocks, first_blocks, second_blocks])
    key_ids = jnp.concatenate([own_blocks, second_blocks, first_blocks])
    tile_kind = jnp.concatenate([jnp.zeros((block_count,), jnp.int32), jnp.ones((pair_count,), jnp.int32), jnp.full((pair_count,), 2, jnp.int32)])
    tile_total = query_ids.shape[0]
    group_size = 64
    padding = (-tile_total) % group_size
    filler = jnp.zeros((padding,), jnp.int32)
    dummy = jnp.full((padding,), block_count, jnp.int32)
    query_pad = jnp.concatenate([query_ids, filler]).reshape(-1, group_size)
    key_pad = jnp.concatenate([key_ids, filler]).reshape(-1, group_size)
    query_seg = jnp.concatenate([query_ids, dummy]).reshape(-1, group_size)
    key_seg = jnp.concatenate([key_ids, dummy]).reshape(-1, group_size)
    kind_pad = jnp.concatenate([tile_kind, filler]).reshape(-1, group_size)

    def lse_of(tile_args):
        query_group, key_group = tile_args
        return tile_forward(queries[query_group], keys[key_group], values[key_group])[1]

    all_lse = lax.map(lse_of, (query_pad, key_pad)).reshape(-1, head_count, block_rows)
    flat_seg = query_seg.reshape(-1)
    seg_top = jax.ops.segment_max(all_lse, flat_seg, num_segments=block_count + 1)
    seg_total = jax.ops.segment_sum(jnp.exp(all_lse - seg_top[flat_seg]), flat_seg, num_segments=block_count + 1)
    block_lse = seg_top + jnp.log(seg_total)

    def add_part(accumulated, tile_args):
        query_group, key_group, seg_group = tile_args
        tile_part, tile_lse = tile_forward(queries[query_group], keys[key_group], values[key_group])
        weight = jnp.exp(tile_lse - block_lse[seg_group])
        scaled = tile_part.reshape(group_size, head_count, HEAD, block_rows) * weight[:, :, None, :]
        return accumulated.at[seg_group].add(scaled), None

    start_acc = jnp.zeros((block_count + 1, head_count, HEAD, block_rows), jnp.float32)
    accumulated, _ = lax.scan(add_part, start_acc, (query_pad, key_pad, query_seg))
    attention = accumulated[:block_count]
    attn_low = attention.astype(jnp.bfloat16).reshape(block_count, feature_count, block_rows)
    out = jnp.einsum("bfr,fo->bro", attn_low.astype(jnp.float32), out_weight.astype(jnp.float32)).astype(jnp.bfloat16)
    attn_grad = jnp.einsum("bro,fo->bfr", out_grad.astype(jnp.float32), out_weight.astype(jnp.float32)).astype(jnp.bfloat16)
    row_delta = jnp.sum(attn_grad.astype(jnp.float32).reshape(block_count, head_count, HEAD, block_rows) * attention, axis=2)
    grad_pad = jnp.concatenate([attn_grad, jnp.zeros_like(attn_grad[:1])])
    lse_pad = block_lse
    delta_pad = jnp.concatenate([row_delta, jnp.zeros_like(row_delta[:1])])

    def add_grads(carried, tile_args):
        sum_q, sum_k, sum_v = carried
        query_group, key_group, qseg_group, kseg_group, kind_group = tile_args
        term_q, term_k, term_v = tile_backward(queries[query_group], keys[key_group], values[key_group], grad_pad[query_group], lse_pad[query_group], delta_pad[query_group])
        term_q = jnp.where((kind_group == 2)[:, None, None], lowered(term_q), term_q)
        term_k = jnp.where((kind_group > 0)[:, None, None], lowered(term_k), term_k)
        term_v = jnp.where((kind_group > 0)[:, None, None], lowered(term_v), term_v)
        return (sum_q.at[qseg_group].add(term_q), sum_k.at[kseg_group].add(term_k), sum_v.at[kseg_group].add(term_v)), None

    zero_grad = jnp.zeros((block_count + 1, feature_count, block_rows), jnp.float32)
    sums, _ = lax.scan(add_grads, (zero_grad, zero_grad, zero_grad), (query_pad, key_pad, query_seg, key_seg, kind_pad))
    grad_q = sums[0][:block_count].astype(jnp.bfloat16)
    grad_k = sums[1][:block_count].astype(jnp.bfloat16)
    grad_v = sums[2][:block_count].astype(jnp.bfloat16)
    return (out, grad_q, grad_k, grad_v)
```

```python
import functools

import jax
import jax.numpy as jnp
from jax import lax
from jax.experimental import pallas as pl
from jax.experimental.pallas import tpu as pltpu
from jax.sharding import PartitionSpec as P

MESH = pl.DeviceIdType.MESH
HEAD = 32
NY, NZ, NX = 4, 8, 4
BLK = 16
PART_A = 10
PART_B = BLK - PART_A
BASE_B = 2 * NY * NZ * PART_A
SLOTS = 2 * NY * NZ * BLK
UNROLL = 4
LIST = 192
NEG = -1e30
RATE = HEAD**-0.5 * 1.4426950408889634
SCALE = HEAD**-0.5
F32 = jnp.float32
BF16 = jnp.bfloat16


def place():
    blk, hd = lax.axis_index("blk"), lax.axis_index("hd")
    core, z, y = blk % 2, (blk // 2) % NZ, blk // (2 * NZ)

    def device(yy, zz, cc, xx):
        return ((yy * NZ + zz) * 2 + cc, xx)

    return y, z, core, hd, device


def slot_of(block):
    dev, inner = block // BLK, block % BLK
    core, z, y = dev % 2, (dev // 2) % NZ, dev // (2 * NZ)
    in_a = ((core * NY + y) * NZ + z) * PART_A + inner
    in_b = BASE_B + ((core * NZ + z) * NY + y) * PART_B + inner - PART_A
    return jnp.where(inner < PART_A, in_a, in_b)


def meet(peers):
    barrier = pltpu.get_barrier_semaphore()
    for peer in peers:
        pl.semaphore_signal(barrier, inc=1, device_id=peer, device_id_type=MESH)
    pl.semaphore_wait(barrier, len(peers))


class Gather:
    SEMS = 48

    def __init__(self, buffer, send_sem, recv_sem, coords, base=0):
        self.buffer, self.send_sem, self.recv_sem = buffer, send_sem, recv_sem
        self.y, self.z, self.core, hd, device = coords
        y, z, core = self.y, self.z, self.core
        self.z_next, self.z_last = device(y, (z + 1) % NZ, core, hd), device(y, (z + NZ - 1) % NZ, core, hd)
        self.y_next, self.y_last = device((y + 1) % NY, z, core, hd), device((y + NY - 1) % NY, z, core, hd)
        self.twin = device(y, z, 1 - core, hd)
        self.base = base
        self.sent = []

    def peers(self):
        return [self.z_next, self.z_last, self.y_next, self.y_last, self.twin]

    def rows_a(self, core, y, z, start, count):
        return self.buffer.at[pl.ds(((core * NY + y) * NZ + z) * PART_A + start, count)]

    def rows_b(self, core, z, y, start, count):
        return self.buffer.at[pl.ds(BASE_B + ((core * NZ + z) * NY + y) * PART_B + start, count)]

    def own(self):
        return (
            self.rows_a(self.core, self.y, self.z, 0, PART_A),
            self.rows_b(self.core, self.z, self.y, 0, PART_B),
        )

    def copy(self, rows, peer, sem):
        sem += self.base
        return pltpu.make_async_remote_copy(
            src_ref=rows, dst_ref=rows, send_sem=self.send_sem.at[sem], recv_sem=self.recv_sem.at[sem],
            device_id=peer, device_id_type=MESH)

    def leg(self, kind, step, way, arriving):
        hop = step + 1 if arriving else step
        sign = -1 if way == 0 else 1
        zz, yy = (self.z + sign * hop + 2 * NZ) % NZ, (self.y + sign * hop + 2 * NY) % NY
        core = self.core
        if kind == "az":
            half = PART_A // 2
            rows = self.rows_a(core, self.y, zz, 0, PART_A) if step < 3 else self.rows_a(core, self.y, zz, way * half, half)
            sem = 0 + 2 * step + way
        elif kind == "by":
            half = PART_B // 2
            rows = self.rows_b(core, self.z, yy, 0, PART_B) if step < 1 else self.rows_b(core, self.z, yy, way * half, half)
            sem = 8 + 2 * step + way
        elif kind == "ay":
            rows = self.rows_a(core, yy, 0, 0, NZ * PART_A) if step < 1 else self.rows_a(core, yy, 4 * way, 0, 4 * PART_A)
            sem = 12 + 2 * step + way
        else:
            rows = self.rows_b(core, zz, 0, 0, NY * PART_B) if step < 3 else self.rows_b(core, zz, 2 * way, 0, 2 * PART_B)
            sem = 16 + 2 * step + way
        along_z = kind in ("az", "bz")
        peer = (self.z_next if way == 0 else self.z_last) if along_z else (self.y_next if way == 0 else self.y_last)
        return self.copy(rows, peer, sem)

    def send(self, kind, step):
        for way in (0, 1):
            leg = self.leg(kind, step, way, False)
            leg.start()
            self.sent.append(leg)

    def forward(self, kind, step):
        for way in (0, 1):
            self.leg(kind, step, way, True).wait_recv()
            leg = self.leg(kind, step + 1, way, False)
            leg.start()
            self.sent.append(leg)

    def arrive(self, kind, step):
        for way in (0, 1):
            self.leg(kind, step, way, True).wait_recv()

    def twin_a(self, hop, core):
        return self.copy(self.rows_a(core, (self.y + hop + NY) % NY, 0, 0, NZ * PART_A), self.twin, 24 + hop % NY)

    def twin_b(self, hop, core):
        return self.copy(self.rows_b(core, (self.z + hop + NZ) % NZ, 0, 0, NY * PART_B), self.twin, 28 + hop % NZ)

    def pass_on(self, which, *hops):
        for hop in hops:
            leg = which(hop, self.core)
            leg.start()
            self.sent.append(leg)

    def steps(self):
        return [
            lambda: (self.send("az", 0), self.send("by", 0)),
            lambda: self.forward("by", 0),
            lambda: self.forward("az", 0),
            lambda: (self.arrive("by", 1), self.send("bz", 0), self.pass_on(self.twin_b, 0)),
            lambda: self.forward("az", 1),
            lambda: self.forward("az", 2),
            lambda: (self.arrive("az", 3), self.send("ay", 0), self.pass_on(self.twin_a, 0)),
            lambda: (self.forward("bz", 0), self.pass_on(self.twin_b, -1, 1)),
            lambda: (self.forward("bz", 1), self.pass_on(self.twin_b, -2, 2)),
            lambda: (self.forward("ay", 0), self.pass_on(self.twin_a, -1, 1)),
            lambda: (self.forward("bz", 2), self.pass_on(self.twin_b, -3, 3)),
            lambda: (self.arrive("ay", 1), self.pass_on(self.twin_a, 2)),
            lambda: (self.arrive("bz", 3), self.pass_on(self.twin_b, 4)),
            self.finish,
        ]

    def finish(self):
        for hop in range(NY):
            self.twin_a(hop, 1 - self.core).wait_recv()
        for hop in range(NZ):
            self.twin_b(hop, 1 - self.core).wait_recv()
        for leg in self.sent:
            leg.wait_send()


def gather_kernel(k_ref, v_ref, q_ref, g_ref, kv_ref, qg_ref, local_sem, send_sem, recv_sem):
    coords = place()
    kv = Gather(kv_ref, send_sem, recv_sem, coords)
    qg = Gather(qg_ref, send_sem, recv_sem, coords, Gather.SEMS)
    copies = []
    for number, (gather, refs) in enumerate(((kv, (k_ref, v_ref)), (qg, (q_ref, g_ref)))):
        for side, ref in enumerate(refs):
            rows_a, rows_b = gather.own()
            features = pl.ds(64 * side, 64)
            copies.append(pltpu.make_async_copy(ref.at[pl.ds(0, PART_A)], rows_a.at[:, features], local_sem.at[4 * number + 2 * side]))
            copies.append(pltpu.make_async_copy(ref.at[pl.ds(PART_A, PART_B)], rows_b.at[:, features], local_sem.at[4 * number + 2 * side + 1]))
    for copy in copies:
        copy.start()
    meet(kv.peers())
    for copy in copies:
        copy.wait()
    for step in kv.steps()[:-1]:
        step()
    for step in qg.steps()[:-1]:
        step()
    kv.finish()
    qg.finish()


def gather_all(keys, values, queries, grads):
    shape = jax.ShapeDtypeStruct((SLOTS, 128, 128), BF16)
    sem = pltpu.SemaphoreType.DMA
    anywhere = pl.BlockSpec(memory_space=pl.ANY)
    return pl.pallas_call(
        gather_kernel, out_shape=(shape, shape), in_specs=[anywhere] * 4, out_specs=(anywhere,) * 2,
        scratch_shapes=[sem((8,)), sem((2 * Gather.SEMS,)), sem((2 * Gather.SEMS,))],
        compiler_params=pltpu.CompilerParams(collective_id=0, has_side_effects=True),
        name="gather_rows",
    )(keys, values, queries, grads)


def spread(first, second):
    parts = (first[:HEAD], first[HEAD:], second[:HEAD], second[HEAD:])
    zero = jnp.zeros((HEAD, 128), first.dtype)
    rows = [jnp.concatenate([part if col == row else zero for col in range(4)], axis=1) for row, part in enumerate(parts)]
    return jnp.concatenate(rows, axis=0)


def diagonal(full, top):
    return full[top:top + HEAD, :128], full[top + HEAD:top + 2 * HEAD, 128:]


def dot(a, b):
    return jnp.dot(a, b, preferred_element_type=F32)


def dot_nt(a, b):
    return lax.dot_general(a, b, (((1,), (1,)), ((), ())), preferred_element_type=F32)


def query_tile(kv, right):
    both = dot(kv.T, right)
    scores, prob_grad = both[:, :256], both[:, 256:]
    top = jnp.max(scores, axis=0, keepdims=True)
    expo = jnp.exp2((scores - top) * RATE)
    total = jnp.sum(expo, axis=0, keepdims=True)
    weighed = jnp.sum(expo * prob_grad, axis=0, keepdims=True)
    mean = weighed / total
    change = (expo * (prob_grad - mean)).astype(BF16)
    by_expo = dot(kv, expo.astype(BF16))
    by_change = dot(kv[:64], change)
    heads = []
    for h in range(2):
        cols = slice(128 * h, 128 * h + 128)
        b = diagonal(by_expo, 0)[h]
        o = diagonal(by_expo, 64)[h]
        a = diagonal(by_change, 0)[h] + mean[:, cols] * b
        heads.append((top[:, cols], total[:, cols], weighed[:, cols], o, a, b))
    return heads


def query_merge(old, new, reset, skip):
    merged = []
    for (m0, *acc), (m1, *add) in zip(old, new):
        m0, m1 = m0 + reset, m1 + skip
        m = jnp.maximum(m0, m1)
        w0, w1 = jnp.exp2((m0 - m) * RATE), jnp.exp2((m1 - m) * RATE)
        merged.append((m, *[x * w0 + y * w1 for x, y in zip(acc, add)]))
    return merged


def query_result(state):
    rows, grads, stats = [], [], []
    for m, total, weighed, o, a, b in state:
        inverse = 1.0 / total
        delta = weighed * inverse
        rows.append((o * inverse).astype(BF16))
        grads.append(((a - delta * b) * (inverse * SCALE)).astype(BF16))
        stats.append((m + jnp.log2(total) * (1.0 / RATE), delta))
    aux = [stats[0][0], stats[1][0], stats[0][1], stats[1][1], jnp.zeros((4, 128), F32)]
    return jnp.concatenate(rows, axis=0), jnp.concatenate(grads, axis=0), jnp.concatenate(aux, axis=0)


def zero_state():
    row, block = jnp.zeros((1, 128), F32), jnp.zeros((HEAD, 128), F32)
    return [(row, row, row, block, block, block) for _ in range(2)]


def fetch(source, buffer, sem, list_ref, group):
    for u in range(UNROLL):
        yield pltpu.make_async_copy(
            source.at[list_ref[group * UNROLL + u] % SLOTS], buffer.at[lax.rem(group, 2), u], sem.at[lax.rem(group, 2), u])


def query_kernel(list_ref, count_ref, q_ref, g_ref, kv_hbm, attn_ref, grad_ref, aux_ref, right, buffer, sem):
    count = count_ref[0]
    groups = (count + UNROLL - 1) // UNROLL
    for copy in fetch(kv_hbm, buffer, sem, list_ref, 0):
        copy.start()
    for x in range(BLK):
        right[x] = spread(q_ref[x], g_ref[x])

    def body(group, state):
        @pl.when(group + 1 < groups)
        def _():
            for copy in fetch(kv_hbm, buffer, sem, list_ref, group + 1):
                copy.start()

        for copy in fetch(kv_hbm, buffer, sem, list_ref, group):
            copy.wait()
        tiles = []
        for u in range(UNROLL):
            t = group * UNROLL + u
            tiles.append(query_tile(buffer[lax.rem(group, 2), u], right[list_ref[t] // SLOTS]))
        for u in range(UNROLL):
            t = group * UNROLL + u
            x = list_ref[t] // SLOTS
            before = list_ref[jnp.maximum(t - 1, 0)] // SLOTS
            reset = jnp.where((t == 0) | (before != x), NEG, 0.0).astype(F32)
            skip = jnp.where(t < count, 0.0, NEG).astype(F32)
            state = query_merge(state, tiles[u], reset, skip)
            rows, grads, aux = query_result(state)
            attn_ref[x] = rows
            grad_ref[x] = grads
            aux_ref[x] = aux
        return state

    lax.fori_loop(0, groups, body, zero_state())


def key_kernel(list_ref, count_ref, k_ref, v_ref, aux_all, qg_hbm, dk_ref, dv_ref, left, buffer, aux_buf, sem, aux_sem):
    count = count_ref[0]
    groups = (count + UNROLL - 1) // UNROLL

    def copies(group):
        yield from fetch(qg_hbm, buffer, sem, list_ref, group)
        yield from fetch(aux_all, aux_buf, aux_sem, list_ref, group)

    for copy in copies(0):
        copy.start()
    for y in range(BLK):
        left[y] = jnp.concatenate([k_ref[y], v_ref[y]], axis=0).T

    def body(group, state):
        @pl.when(group + 1 < groups)
        def _():
            for copy in copies(group + 1):
                copy.start()

        for copy in copies(group):
            copy.wait()
        terms = []
        for u in range(UNROLL):
            t = group * UNROLL + u
            terms.append(key_tile(left[list_ref[t] // SLOTS], buffer[lax.rem(group, 2), u], aux_buf[lax.rem(group, 2), u]))
        for u in range(UNROLL):
            t = group * UNROLL + u
            y = list_ref[t] // SLOTS
            before = list_ref[jnp.maximum(t - 1, 0)] // SLOTS
            keep = jnp.where((t == 0) | (before != y), 0.0, 1.0).astype(F32)
            use = jnp.where(t < count, 1.0, 0.0).astype(F32)
            state = tuple(x * keep + z * use for x, z in zip(state, terms[u]))
            dk_ref[y] = (state[0] * SCALE).astype(BF16)
            dv_ref[y] = state[1].astype(BF16)
        return state

    zero = jnp.zeros((64, 128), F32)
    lax.fori_loop(0, groups, body, (zero, zero))


def key_tile(left, qg, aux):
    right = spread(qg[:64], qg[64:])
    both = dot(left, right)
    lse = jnp.concatenate([aux[0:1], aux[1:2]], axis=1)
    delta = jnp.concatenate([aux[2:3], aux[3:4]], axis=1)
    prob = jnp.exp2((both[:, :256] - lse) * RATE)
    change = (prob * (both[:, 256:] - delta)).astype(BF16)
    term_k = dot_nt(right[:64, :256], change)
    term_v = dot_nt(right[64:, 256:], prob.astype(BF16))
    return term_k, term_v


def share_kernel(attn_ref, w_ref, aux_ref, out_ref, all_ref, local_sem, send_sem, recv_sem, outgoing, incoming):
    coords = place()
    y, z, core, hd, device = coords
    gather = Gather(all_ref, send_sem, recv_sem, coords)
    rows_a, rows_b = gather.own()
    copies = [
        pltpu.make_async_copy(aux_ref.at[pl.ds(0, PART_A)], rows_a, local_sem.at[0]),
        pltpu.make_async_copy(aux_ref.at[pl.ds(PART_A, PART_B)], rows_b, local_sem.at[1]),
    ]
    for copy in copies:
        copy.start()
    partners = [device(y, z, core, (hd + hop) % NX) for hop in range(1, NX)]
    meet(gather.peers() + partners)
    for copy in copies:
        copy.wait()
    steps = gather.steps()
    for step in steps[:3]:
        step()

    def project(a, carry):
        part = lax.dot_general(attn_ref[a], w_ref[...], (((0,), (0,)), ((), ())), preferred_element_type=F32).astype(BF16)
        for x in range(NX):
            outgoing[x, a] = part[32 * x:32 * x + 32]
        return carry

    lax.fori_loop(0, BLK, project, 0)
    legs = []
    for hop in range(1, NX):
        to = (hd + hop) % NX
        leg = pltpu.make_async_remote_copy(
            src_ref=outgoing.at[to], dst_ref=incoming.at[hop - 1], send_sem=send_sem.at[Gather.SEMS + hop],
            recv_sem=recv_sem.at[Gather.SEMS + hop], device_id=partners[hop - 1], device_id_type=MESH)
        leg.start()
        legs.append(leg)
    for step in steps[3:]:
        step()
    for leg in legs:
        leg.wait()

    def total(a, carry):
        value = outgoing[hd, a].astype(F32)
        for hop in range(NX - 1):
            value += incoming[hop, a].astype(F32)
        out_ref[a] = value.astype(BF16)
        return carry

    lax.fori_loop(0, BLK, total, 0)


def tile_list(pair_list):
    me = lax.axis_index("blk")
    first, second = pair_list[0], pair_list[1]
    count_all = first.shape[0]
    mine = count_all // lax.axis_size("blk")
    start = me * BLK
    own = start + jnp.arange(BLK, dtype=jnp.int32)
    out_first = lax.dynamic_slice_in_dim(first, me * mine, mine)
    out_second = lax.dynamic_slice_in_dim(second, me * mine, mine)
    near = jnp.concatenate([own, out_first, second])
    far = jnp.concatenate([own, out_second, first])
    inside = (near >= start) & (near < start + BLK)
    number = near.shape[0]
    order = jnp.where(inside, near - start, BLK) * 4096 + jnp.arange(number, dtype=jnp.int32)
    rank = jnp.sum((order[None, :] < order[:, None]).astype(jnp.int32), axis=1)
    rank = jnp.where(inside, rank, LIST)
    value = (near - start) * SLOTS + slot_of(far)
    hit = rank[None, :] == jnp.arange(LIST, dtype=jnp.int32)[:, None]
    entries = jnp.sum(jnp.where(hit, value[None, :], 0), axis=1)
    count = jnp.sum(inside.astype(jnp.int32))
    entries = jnp.where(jnp.arange(LIST) < count, entries, (BLK - 1) * SLOTS)
    return entries.astype(jnp.int32), count[None].astype(jnp.int32)


def local(queries, keys, values, out_weight, out_grad, pair_list):
    entries, count = tile_list(pair_list)
    grads = jnp.einsum("bro,fo->bfr", out_grad, out_weight, preferred_element_type=F32).astype(BF16)
    kv_all, qg_all = gather_all(keys, values, queries, grads)
    smem = pl.BlockSpec(memory_space=pltpu.SMEM)
    vmem = pl.BlockSpec(memory_space=pltpu.VMEM)
    anywhere = pl.BlockSpec(memory_space=pl.ANY)
    sem = pltpu.SemaphoreType.DMA
    half = jax.ShapeDtypeStruct((BLK, 64, 128), BF16)
    attn, grad_q, aux = pl.pallas_call(
        query_kernel,
        out_shape=(half, half, jax.ShapeDtypeStruct((BLK, 8, 128), F32)),
        in_specs=[smem, smem, vmem, vmem, anywhere], out_specs=(vmem,) * 3,
        scratch_shapes=[pltpu.VMEM((BLK, 128, 512), BF16), pltpu.VMEM((2, UNROLL, 128, 128), BF16), sem((2, UNROLL))],
        compiler_params=pltpu.CompilerParams(vmem_limit_bytes=32 * 2**20),
        name="query_side",
    )(entries, count, queries, grads, kv_all)
    out, aux_all = pl.pallas_call(
        share_kernel,
        out_shape=(jax.ShapeDtypeStruct((BLK, 32, 256), BF16), jax.ShapeDtypeStruct((SLOTS, 8, 128), F32)),
        in_specs=[vmem, vmem, vmem], out_specs=(vmem, anywhere),
        scratch_shapes=[sem((2,)), sem((Gather.SEMS + NX,)), sem((Gather.SEMS + NX,)), pltpu.VMEM((NX, BLK, 32, 256), BF16),
                        pltpu.VMEM((NX - 1, BLK, 32, 256), BF16)],
        compiler_params=pltpu.CompilerParams(collective_id=1, has_side_effects=True, vmem_limit_bytes=32 * 2**20),
        name="share_rows",
    )(attn, out_weight, aux)
    grad_k, grad_v = pl.pallas_call(
        key_kernel,
        out_shape=(half, half),
        in_specs=[smem, smem, vmem, vmem, anywhere, anywhere], out_specs=(vmem,) * 2,
        scratch_shapes=[pltpu.VMEM((BLK, 128, 128), BF16), pltpu.VMEM((2, UNROLL, 128, 128), BF16),
                        pltpu.VMEM((2, UNROLL, 8, 128), F32), sem((2, UNROLL)), sem((2, UNROLL))],
        compiler_params=pltpu.CompilerParams(vmem_limit_bytes=32 * 2**20),
        name="key_side",
    )(entries, count, keys, values, aux_all, qg_all)
    return out, grad_q, grad_k, grad_v


def solution(mesh):
    blocks, weight = P("blk", "hd", None), P("hd", None)
    return jax.shard_map(
        local, mesh=mesh,
        in_specs=(blocks, blocks, blocks, weight, P("blk", None, None), P()),
        out_specs=(blocks,) * 4, check_vma=False)
```

```python
import functools

import jax
import jax.numpy as jnp
from jax import lax
from jax.experimental import pallas as pl
from jax.experimental.pallas import tpu as pltpu
from jax.sharding import PartitionSpec as P

MESH = pl.DeviceIdType.MESH
HEAD = 32
NY, NZ, NX = 4, 8, 4
BLK = 16
COLUMN = 2 * NZ * BLK
UNROLL = 4
NEG = -1e30
RATE = HEAD**-0.5 * 1.4426950408889634
SCALE = HEAD**-0.5
F32 = jnp.float32
BF16 = jnp.bfloat16
VMEM_LIMIT = 60 * 2**20


def place():
    blk, hd = lax.axis_index("blk"), lax.axis_index("hd")
    core, z, y = blk % 2, (blk // 2) % NZ, blk // (2 * NZ)

    def device(yy, zz, cc, xx):
        return ((yy * NZ + zz) * 2 + cc, xx)

    return y, z, core, hd, device


def meet(peers):
    barrier = pltpu.get_barrier_semaphore()
    for peer in peers:
        pl.semaphore_signal(barrier, inc=1, device_id=peer, device_id_type=MESH)
    pl.semaphore_wait(barrier, len(peers))


class Sems:
    def __init__(self, send, recv):
        self.send, self.recv, self.used = send, recv, 0

    def take(self, count):
        self.used += count
        return self.used - count

    def copy(self, source, target, peer, sem):
        return pltpu.make_async_remote_copy(
            src_ref=source, dst_ref=target, send_sem=self.send.at[sem], recv_sem=self.recv.at[sem],
            device_id=peer, device_id_type=MESH)


class Ring:
    def __init__(self, buffer, coords, sems, pieces):
        self.buffer, self.sems, self.pieces = buffer, sems, pieces
        y, z, core, hd, device = coords
        self.z, self.core = z, core
        self.peer = (device(y, (z + 1) % NZ, core, hd), device(y, (z + NZ - 1) % NZ, core, hd))
        self.twin = device(y, z, 1 - core, hd)
        self.size = BLK // pieces
        self.leg_sem, self.twin_sem = sems.take(8 * pieces), sems.take(8 * pieces)
        self.sent = []

    def peers(self):
        return [*self.peer, self.twin]

    def rows(self, z, core, start, count):
        return self.buffer.at[pl.ds((z * 2 + core) * BLK + start, count)]

    def leg(self, piece, step, way, arriving):
        hop = step + 1 if arriving else step
        z = (self.z - hop + NZ) % NZ if way == 0 else (self.z + hop) % NZ
        start, count = piece * self.size, self.size
        if step == 3:
            count //= 2
            start += way * count
        rows = self.rows(z, self.core, start, count)
        return self.sems.copy(rows, rows, self.peer[way], self.leg_sem + (piece * 4 + step) * 2 + way)

    def pass_on(self, piece, hop, core):
        rows = self.rows((self.z + hop + NZ) % NZ, core, piece * self.size, self.size)
        return self.sems.copy(rows, rows, self.twin, self.twin_sem + piece * 8 + hop % NZ)

    def go(self, copy):
        copy.start()
        self.sent.append(copy)

    def start(self):
        for piece in range(self.pieces):
            for way in (0, 1):
                self.go(self.leg(piece, 0, way, False))
        for piece in range(self.pieces):
            self.go(self.pass_on(piece, 0, self.core))

    def advance(self, step):
        for piece in range(self.pieces):
            for way in (0, 1):
                self.leg(piece, step, way, True).wait_recv()
                if step < 3:
                    self.go(self.leg(piece, step + 1, way, False))
                    self.go(self.pass_on(piece, -1 - step if way == 0 else 1 + step, self.core))
            if step == 3:
                self.go(self.pass_on(piece, 4, self.core))

    def arrive(self):
        for piece in range(self.pieces):
            for hop in range(NZ):
                self.pass_on(piece, hop, 1 - self.core).wait_recv()

    def drain(self):
        for copy in self.sent:
            copy.wait_send()


class Cross:
    def __init__(self, send, relay, recv, cap, coords, sems):
        self.send, self.relay, self.recv, self.cap, self.sems = send, relay, recv, cap, sems
        y, z, core, hd, device = coords
        self.peer = (device((y + 1) % NY, z, core, hd), device((y + NY - 1) % NY, z, core, hd))
        self.sem = sems.take(6)
        self.sent = []

    def peers(self):
        return [*self.peer]

    def first(self, way):
        half = self.cap // 2
        return self.sems.copy(
            self.send.at[pl.ds(self.cap + way * half, half)], self.relay.at[pl.ds(way * half, half)], self.peer[way], self.sem + way)

    def second(self, way):
        half = self.cap // 2
        return self.sems.copy(
            self.relay.at[pl.ds(way * half, half)], self.recv.at[pl.ds(2 * self.cap + way * half, half)], self.peer[way],
            self.sem + 2 + way)

    def direct(self, way):
        return self.sems.copy(
            self.send.at[pl.ds(2 * way * self.cap, self.cap)],
            self.recv.at[pl.ds((3 - 2 * way) * self.cap, self.cap)], self.peer[way], self.sem + 4 + way)

    def go(self, copy):
        copy.start()
        self.sent.append(copy)

    def pack(self, column, list_ref):
        def move(hop, target, base):
            def body(step, carry):
                for u in range(4):
                    row = step * 4 + u
                    target[base + row] = column[list_ref[hop * self.cap + row]]
                return carry

            lax.fori_loop(0, self.cap // 4, body, 0)

        move(2, self.send, self.cap)
        for way in (0, 1):
            self.go(self.first(way))
        move(1, self.send, 0)
        self.go(self.direct(0))
        move(3, self.send, 2 * self.cap)
        self.go(self.direct(1))
        move(0, self.recv, 0)

    def relay_on(self):
        for way in (0, 1):
            self.first(way).wait_recv()
            self.go(self.second(way))

    def arrive(self):
        for way in (0, 1):
            self.direct(way).wait_recv()
            self.second(way).wait_recv()

    def drain(self):
        for copy in self.sent:
            copy.wait_send()


def spread(first, second):
    parts = (first[:HEAD], first[HEAD:], second[:HEAD], second[HEAD:])
    zero = jnp.zeros((HEAD, 128), first.dtype)
    rows = [jnp.concatenate([part if col == row else zero for col in range(4)], axis=1) for row, part in enumerate(parts)]
    return jnp.concatenate(rows, axis=0)


def diagonal(full, top):
    return full[top:top + HEAD, :128], full[top + HEAD:top + 2 * HEAD, 128:]


def dot(a, b):
    return jnp.dot(a, b, preferred_element_type=F32)


def dot_nt(a, b):
    return lax.dot_general(a, b, (((1,), (1,)), ((), ())), preferred_element_type=F32)


def query_tile(kv, right):
    both = dot(kv.T, right)
    scores, prob_grad = both[:, :256], both[:, 256:]
    top = jnp.max(scores, axis=0, keepdims=True)
    expo = jnp.exp2((scores - top) * RATE)
    total = jnp.sum(expo, axis=0, keepdims=True)
    weighed = jnp.sum(expo * prob_grad, axis=0, keepdims=True)
    mean = weighed / total
    change = (expo * (prob_grad - mean)).astype(BF16)
    by_expo = dot(kv, expo.astype(BF16))
    by_change = dot(kv[:64], change)
    heads = []
    for h in range(2):
        cols = slice(128 * h, 128 * h + 128)
        b = diagonal(by_expo, 0)[h]
        o = diagonal(by_expo, 64)[h]
        a = diagonal(by_change, 0)[h] + mean[:, cols] * b
        heads.append((top[:, cols], total[:, cols], weighed[:, cols], o, a, b))
    return heads


def query_merge(old, new, skip):
    merged = []
    for (m0, *acc), (m1, *add) in zip(old, new):
        m1 = m1 + skip
        m = jnp.maximum(m0, m1)
        w0, w1 = jnp.exp2((m0 - m) * RATE), jnp.exp2((m1 - m) * RATE)
        merged.append((m, *[x * w0 + y * w1 for x, y in zip(acc, add)]))
    return merged


def query_result(state):
    rows, grads, stats = [], [], []
    for m, total, weighed, o, a, b in state:
        inverse = 1.0 / total
        delta = weighed * inverse
        rows.append((o * inverse).astype(BF16))
        grads.append(((a - delta * b) * (inverse * SCALE)).astype(BF16))
        stats.append((m + jnp.log2(total) * (1.0 / RATE), delta))
    aux = [stats[0][0], stats[1][0], stats[0][1], stats[1][1], jnp.zeros((4, 128), F32)]
    return jnp.concatenate(rows + grads, axis=0), jnp.concatenate(aux, axis=0)


def pack_state(state):
    rows = [x for head in state for x in head[:3]] + [jnp.zeros((2, 128), F32)]
    return jnp.concatenate(rows, axis=0), jnp.concatenate([x for head in state for x in head[3:]], axis=0)


def load_state(rows, blocks):
    return [
        (*[rows[3 * h + i:3 * h + i + 1] for i in range(3)], *[blocks[96 * h + 32 * i:96 * h + 32 * i + 32] for i in range(3)])
        for h in range(2)
    ]


def key_tile(left, qg, aux):
    right = spread(qg[:64], qg[64:])
    both = dot(left, right)
    lse = jnp.concatenate([aux[0:1], aux[1:2]], axis=1)
    delta = jnp.concatenate([aux[2:3], aux[3:4]], axis=1)
    prob = jnp.exp2((both[:, :256] - lse) * RATE)
    change = (prob * (both[:, 256:] - delta)).astype(BF16)
    term_k = dot_nt(right[:64, :256], change)
    term_v = dot_nt(right[64:, 256:], prob.astype(BF16))
    return jnp.concatenate([term_k, term_v], axis=0)


def kernel(cap, far, send_list, tile_list, last_list, count_ref, q_ref, k_ref, v_ref, w_ref, og_ref,
           out_ref, dq_ref, dk_ref, dv_ref,
           col_kv, col_qg, col_aux, send_kv, send_qg, send_aux, relay_kv, relay_qg, relay_aux, recv_kv, recv_qg, recv_aux,
           right, left, self_rows, self_blocks, both_t, aux_t, aux_own, attn_own, self_terms,
           outgoing, incoming, send_sem, recv_sem):
    coords = place()
    y, z, core, hd, device = coords
    own = (z * 2 + core) * BLK
    sems = Sems(send_sem, recv_sem)
    ring_kv, ring_qg, ring_aux = (Ring(buffer, coords, sems, pieces) for buffer, pieces in ((col_kv, 2), (col_qg, 2), (col_aux, 1)))
    cross_kv = Cross(send_kv, relay_kv, recv_kv, cap, coords, sems)
    shared = cap > 32
    if shared:
        send_qg = send_kv
    cross_qg = Cross(send_qg, relay_qg, recv_qg, cap, coords, sems)
    cross_aux = Cross(send_aux, relay_aux, recv_aux, cap, coords, sems)
    partners = [device(y, z, core, (hd + hop) % NX) for hop in range(1, NX)]
    count = count_ref[0]

    def fill_kv(x, carry):
        kv = jnp.concatenate([k_ref[x], v_ref[x]], axis=0)
        col_kv[own + x] = kv
        return carry

    lax.fori_loop(0, BLK, fill_kv, 0)
    meet(ring_kv.peers() + cross_kv.peers() + partners)
    ring_kv.start()

    def fill_qg(x, carry):
        g = dot_nt(w_ref[...], og_ref[x]).astype(BF16)
        q = q_ref[x]
        col_qg[own + x] = jnp.concatenate([q, g], axis=0)
        right[x] = spread(q, g)
        left[x] = jnp.concatenate([k_ref[x], v_ref[x]], axis=0).T
        return carry

    lax.fori_loop(0, BLK, fill_qg, 0)

    def self_query(group, carry):
        for u in range(UNROLL):
            x = group * UNROLL + u
            state = query_tile(jnp.concatenate([k_ref[x], v_ref[x]], axis=0), right[x])
            self_rows[x], self_blocks[x] = pack_state(state)
            both_t[far + x], aux_t[far + x] = query_result(state)
        return carry

    ring_kv.advance(0)
    lax.fori_loop(0, 2, self_query, 0)
    ring_kv.advance(1)
    lax.fori_loop(2, 4, self_query, 0)
    ring_kv.advance(2)
    ring_qg.start()
    ring_kv.advance(3)
    ring_kv.arrive()
    cross_kv.pack(col_kv, send_list)
    ring_qg.advance(0)
    cross_kv.relay_on()
    ring_qg.advance(1)
    ring_qg.advance(2)
    ring_qg.advance(3)
    ring_qg.arrive()
    if shared:
        cross_kv.arrive()
        cross_kv.drain()
    cross_qg.pack(col_qg, send_list)
    if not shared:
        cross_kv.arrive()
        cross_kv.drain()

    def entry(t):
        value = tile_list[t]
        x = value // 1024
        before = tile_list[jnp.maximum(t - 1, 0)] // 1024
        return value % 1024, x, (t == 0) | (before != x)

    def far_query(group, state):
        tiles = []
        for u in range(UNROLL):
            row, x, _ = entry(group * UNROLL + u)
            tiles.append(query_tile(recv_kv[row], right[x]))
        for u in range(UNROLL):
            t = group * UNROLL + u
            _, x, fresh = entry(t)
            base = load_state(self_rows[x], self_blocks[x])
            state = [tuple(jnp.where(fresh, b, s) for b, s in zip(head0, head1)) for head0, head1 in zip(base, state)]
            skip = jnp.where(t < count, 0.0, NEG).astype(F32)
            state = query_merge(state, tiles[u], skip)
            both_t[t], aux_t[t] = query_result(state)
        return state

    row, block = jnp.zeros((1, 128), F32), jnp.zeros((HEAD, 128), F32)
    state = [(row, row, row, block, block, block) for _ in range(2)]
    groups = far // UNROLL
    state = lax.fori_loop(0, groups // 2, far_query, state)
    cross_qg.relay_on()
    lax.fori_loop(groups // 2, groups, far_query, state)

    def finish_query(x, carry):
        t = last_list[x]
        aux = aux_t[t]
        aux_own[x] = aux
        col_aux[own + x] = aux
        both = both_t[t]
        dq_ref[x] = both[64:]
        attn_own[x] = both[:64]
        return carry

    lax.fori_loop(0, BLK, finish_query, 0)
    ring_aux.start()

    def project(a, carry):
        part = lax.dot_general(attn_own[a], w_ref[...], (((0,), (0,)), ((), ())), preferred_element_type=F32).astype(BF16)
        for x in range(NX):
            outgoing[x, a] = part[32 * x:32 * x + 32]
        return carry

    lax.fori_loop(0, BLK, project, 0)
    legs = []
    partner_sem = sems.take(NX - 1)
    for hop in range(1, NX):
        leg = sems.copy(outgoing.at[(hd + hop) % NX], incoming.at[hop - 1], partners[hop - 1], partner_sem + hop - 1)
        leg.start()
        legs.append(leg)

    def self_key(group, carry):
        for u in range(UNROLL):
            x = group * UNROLL + u
            terms = key_tile(left[x], col_qg[own + x], aux_own[x])
            self_terms[x] = terms
            both_t[far + x] = terms.astype(BF16)
        return carry

    ring_aux.advance(0)
    lax.fori_loop(0, 2, self_key, 0)
    ring_aux.advance(1)
    lax.fori_loop(2, 4, self_key, 0)
    ring_aux.advance(2)
    ring_aux.advance(3)
    ring_aux.arrive()
    cross_aux.pack(col_aux, send_list)
    cross_aux.relay_on()
    cross_aux.arrive()
    cross_qg.arrive()

    def far_key(group, state):
        tiles = []
        for u in range(UNROLL):
            row, x, _ = entry(group * UNROLL + u)
            tiles.append(key_tile(left[x], recv_qg[row], recv_aux[row]))
        for u in range(UNROLL):
            t = group * UNROLL + u
            _, x, fresh = entry(t)
            use = jnp.where(t < count, 1.0, 0.0).astype(F32)
            state = jnp.where(fresh, self_terms[x], state) + tiles[u] * use
            both_t[t] = state.astype(BF16)
        return state

    lax.fori_loop(0, groups, far_key, jnp.zeros((128, 128), F32))

    def finish_key(x, carry):
        terms = both_t[last_list[x]]
        dk_ref[x] = (terms[:64].astype(F32) * SCALE).astype(BF16)
        dv_ref[x] = terms[64:]
        return carry

    lax.fori_loop(0, BLK, finish_key, 0)
    for leg in legs:
        leg.wait()

    def total(a, carry):
        value = outgoing[hd, a].astype(F32)
        for hop in range(NX - 1):
            value += incoming[hop, a].astype(F32)
        out_ref[a] = value.astype(BF16)
        return carry

    lax.fori_loop(0, BLK, total, 0)
    for part in (ring_kv, ring_qg, ring_aux, cross_qg, cross_aux):
        part.drain()


def run(cap, far, number, send_list, tile_list, last_list, count, *arrays):
    smem = pl.BlockSpec(memory_space=pltpu.SMEM)
    vmem = pl.BlockSpec(memory_space=pltpu.VMEM)
    sem = pltpu.SemaphoreType.DMA
    half = jax.ShapeDtypeStruct((BLK, 64, 128), BF16)

    def wide(rows, second=None):
        second = rows if second is None else second
        return [pltpu.VMEM((rows, 128, 128), BF16), pltpu.VMEM((second, 128, 128), BF16), pltpu.VMEM((rows, 8, 128), F32)]

    scratch = [
        *wide(COLUMN), *wide(3 * cap, 3 * cap if cap <= 32 else 8), *wide(cap), *wide(4 * cap),
        pltpu.VMEM((BLK, 128, 512), BF16), pltpu.VMEM((BLK, 128, 128), BF16),
        pltpu.VMEM((BLK, 8, 128), F32), pltpu.VMEM((BLK, 192, 128), F32),
        pltpu.VMEM((far + BLK, 128, 128), BF16), pltpu.VMEM((far + BLK, 8, 128), F32),
        pltpu.VMEM((BLK, 8, 128), F32), pltpu.VMEM((BLK, 64, 128), BF16),
        pltpu.VMEM((BLK, 128, 128), F32),
        pltpu.VMEM((NX, BLK, 32, 256), BF16), pltpu.VMEM((NX - 1, BLK, 32, 256), BF16),
        sem((108,)), sem((108,)),
    ]
    return pl.pallas_call(
        functools.partial(kernel, cap, far),
        out_shape=(jax.ShapeDtypeStruct((BLK, 32, 256), BF16), half, half, half),
        in_specs=[smem] * 4 + [vmem] * 5, out_specs=(vmem,) * 4, scratch_shapes=scratch,
        compiler_params=pltpu.CompilerParams(collective_id=number, has_side_effects=True, vmem_limit_bytes=VMEM_LIMIT),
        name="attention",
    )(send_list[:, :cap].reshape(-1), tile_list[:far], last_list, count, *arrays)


def before(marks):
    rows, length = marks.shape
    cut = marks.astype(BF16).reshape(rows, length // 128, 128)
    lower = (jnp.arange(128)[:, None] < jnp.arange(128)[None, :]).astype(BF16)
    inside = jnp.einsum("rsc,cd->rsd", cut, lower, preferred_element_type=F32)
    sums = jnp.sum(cut.astype(F32), axis=2)
    ahead = jnp.arange(length // 128)[:, None] < jnp.arange(length // 128)[None, :]
    starts = jnp.sum(jnp.where(ahead[None], sums[:, :, None], 0.0), axis=1)
    return (inside + starts[:, :, None]).astype(jnp.int32).reshape(rows, length), jnp.sum(sums, axis=1).astype(jnp.int32)


def lists(pair_list, cap, far):
    me = lax.axis_index("blk")
    y, rest = me // (2 * NZ), me % (2 * NZ)
    near = jnp.concatenate([pair_list[0], pair_list[1]])
    away = jnp.concatenate([pair_list[1], pair_list[0]])
    near_dev, away_col = near // BLK, away // COLUMN
    hops = jnp.arange(NY, dtype=jnp.int32)
    asked = (near_dev[None] == ((y + hops) % NY * 2 * NZ + rest)[:, None]) & (away_col == y)[None]
    mine = near_dev == me
    source = mine[None] & (away_col[None] == ((y + hops) % NY)[:, None])
    at_block = mine[None] & ((near % BLK)[None] == jnp.arange(BLK, dtype=jnp.int32)[:, None])
    rank, sums = before(jnp.concatenate([asked, source, at_block], axis=0))
    place_of = jnp.arange(cap, dtype=jnp.int32)
    hit = asked[:, None] & (rank[:NY, None] == place_of[None, :, None])
    send_list = jnp.sum(jnp.where(hit, (away % COLUMN)[None, None], 0), axis=2)
    row = jnp.sum(jnp.where(source, rank[NY:2 * NY] + hops[:, None] * cap, 0), axis=0)
    counts = sums[2 * NY:]
    starts = jnp.sum(jnp.where(jnp.arange(BLK)[None, :] < jnp.arange(BLK)[:, None], counts[None, :], 0), axis=1)
    spot = jnp.sum(jnp.where(at_block, rank[2 * NY:] + starts[:, None], 0), axis=0)
    spot = jnp.where(mine, spot, far)
    value = near % BLK * 1024 + row
    chosen = spot[None] == jnp.arange(far, dtype=jnp.int32)[:, None]
    tile_list = jnp.sum(jnp.where(chosen, value[None], 0), axis=1)
    count = jnp.sum(counts)
    tile_list = jnp.where(jnp.arange(far) < count, tile_list, (BLK - 1) * 1024)
    last_list = jnp.where(counts > 0, starts + counts - 1, far + jnp.arange(BLK))
    i32 = jnp.int32
    return send_list.astype(i32), tile_list.astype(i32), last_list.astype(i32), count[None].astype(i32)


def most(pair_list):
    near = jnp.concatenate([pair_list[0], pair_list[1]]) // BLK
    away = jnp.concatenate([pair_list[1], pair_list[0]]) // COLUMN
    bins = jnp.arange(64 * NY, dtype=jnp.int32)
    counts = jnp.sum(((near * NY + away)[None] == bins[:, None]).astype(jnp.int32), axis=1)
    return jnp.max(counts), jnp.max(jnp.sum(counts.reshape(64, NY), axis=1))


def local(queries, keys, values, out_weight, out_grad, pair_list):
    arrays = (queries, keys, values, out_weight, out_grad)

    def branch(cap, far, number):
        return lambda: run(cap, far, number, *lists(pair_list, cap, far), *arrays)

    rows, tiles = most(pair_list)
    return lax.cond((rows <= 32) & (tiles <= 88), branch(32, 88, 0), branch(64, 160, 1))


def solution(mesh):
    blocks, weight = P("blk", "hd", None), P("hd", None)
    return jax.shard_map(
        local, mesh=mesh,
        in_specs=(blocks, blocks, blocks, weight, P("blk", None, None), P()),
        out_specs=(blocks,) * 4, check_vma=False)
```

```python
import functools

import jax
import jax.numpy as jnp
from jax import lax
from jax.experimental import pallas as pl
from jax.experimental.pallas import tpu as pltpu
from jax.sharding import PartitionSpec as P

MESH = pl.DeviceIdType.MESH
HEAD = 32
NY, NZ, NX = 4, 8, 4
BLK = 16
COLUMN = 2 * NZ * BLK
UNROLL = 8
NEG = -1e30
RATE = HEAD**-0.5 * 1.4426950408889634
SCALE = HEAD**-0.5
F32 = jnp.float32
BF16 = jnp.bfloat16
VMEM_LIMIT = 61 * 2**20


def place():
    blk, hd = lax.axis_index("blk"), lax.axis_index("hd")
    core, z, y = blk % 2, (blk // 2) % NZ, blk // (2 * NZ)

    def device(yy, zz, cc, xx):
        return ((yy * NZ + zz) * 2 + cc, xx)

    return y, z, core, hd, device


def meet(peers):
    barrier = pltpu.get_barrier_semaphore()
    for peer in peers:
        pl.semaphore_signal(barrier, inc=1, device_id=peer, device_id_type=MESH)
    pl.semaphore_wait(barrier, len(peers))


class Sems:
    def __init__(self, send, recv):
        self.send, self.recv, self.used = send, recv, 0

    def take(self, count):
        self.used += count
        return self.used - count

    def copy(self, source, target, peer, sem):
        return pltpu.make_async_remote_copy(
            src_ref=source, dst_ref=target, send_sem=self.send.at[sem], recv_sem=self.recv.at[sem],
            device_id=peer, device_id_type=MESH)


class Ring:
    def __init__(self, buffer, coords, sems, pieces):
        self.buffer, self.sems, self.pieces = buffer, sems, pieces
        y, z, core, hd, device = coords
        self.z, self.core = z, core
        self.peer = (device(y, (z + 1) % NZ, core, hd), device(y, (z + NZ - 1) % NZ, core, hd))
        self.twin = device(y, z, 1 - core, hd)
        self.size = BLK // pieces
        self.leg_sem, self.twin_sem = sems.take(8 * pieces), sems.take(8 * pieces)

    def peers(self):
        return [*self.peer, self.twin]

    def rows(self, z, core, start, count):
        return self.buffer.at[pl.ds((z * 2 + core) * BLK + start, count)]

    def leg(self, piece, step, way, arriving):
        hop = step + 1 if arriving else step
        z = (self.z - hop + NZ) % NZ if way == 0 else (self.z + hop) % NZ
        start, count = piece * self.size, self.size
        if step == 3:
            count //= 2
            start += way * count
        rows = self.rows(z, self.core, start, count)
        return self.sems.copy(rows, rows, self.peer[way], self.leg_sem + (piece * 4 + step) * 2 + way)

    def pass_on(self, piece, hop, core):
        rows = self.rows((self.z + hop + NZ) % NZ, core, piece * self.size, self.size)
        return self.sems.copy(rows, rows, self.twin, self.twin_sem + piece * 8 + hop % NZ)

    def start(self):
        for piece in range(self.pieces):
            for way in (0, 1):
                self.leg(piece, 0, way, False).start()
        for piece in range(self.pieces):
            self.pass_on(piece, 0, self.core).start()

    def event(self, step, piece):
        for way in (0, 1):
            self.leg(piece, step, way, True).wait_recv()
            if step < 3:
                self.leg(piece, step + 1, way, False).start()
                self.pass_on(piece, -1 - step if way == 0 else 1 + step, self.core).start()
        if step == 3:
            self.pass_on(piece, 4, self.core).start()

    def advance(self, step):
        for piece in range(self.pieces):
            self.event(step, piece)

    def arrive(self):
        for piece in range(self.pieces):
            for hop in range(NZ):
                self.pass_on(piece, hop, 1 - self.core).wait_recv()

    def drain(self):
        for piece in range(self.pieces):
            for step in range(4):
                for way in (0, 1):
                    self.leg(piece, step, way, False).wait_send()
            for hop in range(NZ):
                self.pass_on(piece, hop, self.core).wait_send()


class Cross:
    def __init__(self, send, relay, recv, cap, coords, sems):
        self.send, self.relay, self.recv, self.cap, self.sems = send, relay, recv, cap, sems
        y, z, core, hd, device = coords
        self.peer = (device((y + 1) % NY, z, core, hd), device((y + NY - 1) % NY, z, core, hd))
        self.sem = sems.take(6)

    def peers(self):
        return [*self.peer]

    def first(self, way):
        half = self.cap // 2
        return self.sems.copy(
            self.send.at[pl.ds(self.cap + way * half, half)], self.relay.at[pl.ds(way * half, half)], self.peer[way], self.sem + way)

    def second(self, way):
        half = self.cap // 2
        return self.sems.copy(
            self.relay.at[pl.ds(way * half, half)], self.recv.at[pl.ds(2 * self.cap + way * half, half)], self.peer[way],
            self.sem + 2 + way)

    def direct(self, way):
        return self.sems.copy(
            self.send.at[pl.ds(2 * way * self.cap, self.cap)],
            self.recv.at[pl.ds((3 - 2 * way) * self.cap, self.cap)], self.peer[way], self.sem + 4 + way)

    def move(self, column, list_ref, hop, target, base):
        def body(step, carry):
            for u in range(2):
                row = step * 2 + u
                target[base + row] = column[list_ref[hop * self.cap + row]]
            return carry

        lax.fori_loop(0, self.cap // 2, body, 0)

    def pack(self, column, list_ref):
        self.move(column, list_ref, 2, self.send, self.cap)
        for way in (0, 1):
            self.first(way).start()
        self.move(column, list_ref, 1, self.send, 0)
        self.direct(0).start()
        self.move(column, list_ref, 3, self.send, 2 * self.cap)
        self.direct(1).start()
        self.move(column, list_ref, 0, self.recv, 0)

    def relay_on(self):
        for way in (0, 1):
            self.first(way).wait_recv()
            self.second(way).start()

    def arrive(self):
        for way in (0, 1):
            self.direct(way).wait_recv()
            self.second(way).wait_recv()

    def drain(self):
        for way in (0, 1):
            self.first(way).wait_send()
            self.direct(way).wait_send()
            self.second(way).wait_send()


class Spray(Cross):
    def __init__(self, send, recv, cap, coords, sems):
        self.send, self.recv, self.cap, self.sems = send, recv, cap, sems
        y, z, core, hd, device = coords
        self.peer = [device((y + hop) % NY, z, core, hd) for hop in range(1, NY)]
        self.sem = sems.take(NY - 1)

    def leg(self, hop):
        return self.sems.copy(
            self.send.at[pl.ds((hop - 1) * self.cap, self.cap)], self.recv.at[pl.ds((NY - hop) * self.cap, self.cap)],
            self.peer[hop - 1], self.sem + hop - 1)

    def pack(self, column, list_ref):
        for hop in (2, 1, 3):
            self.move(column, list_ref, hop, self.send, (hop - 1) * self.cap)
            self.leg(hop).start()
        self.move(column, list_ref, 0, self.recv, 0)

    def arrive(self):
        for hop in range(1, NY):
            self.leg(hop).wait_recv()

    def drain(self):
        for hop in range(1, NY):
            self.leg(hop).wait_send()


def spread(first, second):
    zero = jnp.zeros_like(first)
    return jnp.concatenate([jnp.concatenate([first, zero], axis=1), jnp.concatenate([zero, second], axis=1)], axis=0)


def dot(a, b):
    return jnp.dot(a, b, preferred_element_type=F32)


def dot_nt(a, b):
    return lax.dot_general(a, b, (((1,), (1,)), ((), ())), preferred_element_type=F32)


def query_tile(kv, right):
    both = dot(kv.T, right)
    scores, prob_grad = both[:, :128], both[:, 128:]
    top = jnp.max(scores, axis=0, keepdims=True)
    expo = jnp.exp2((scores - top) * RATE)
    total = jnp.sum(expo, axis=0, keepdims=True)
    weighed = jnp.sum(expo * prob_grad, axis=0, keepdims=True)
    mean = weighed / total
    change = (expo * (prob_grad - mean)).astype(BF16)
    by_expo = dot(kv, expo.astype(BF16))
    by_change = dot(kv[:HEAD], change)
    b, o = by_expo[:HEAD], by_expo[HEAD:]
    return top, total, weighed, o, by_change + mean * b, b


def query_merge(old, new, skip):
    (m0, *acc), (m1, *add) = old, new
    m1 = m1 + skip
    m = jnp.maximum(m0, m1)
    w0, w1 = jnp.exp2((m0 - m) * RATE), jnp.exp2((m1 - m) * RATE)
    return (m, *[x * w0 + y * w1 for x, y in zip(acc, add)])


def query_result(state):
    m, total, weighed, o, a, b = state
    inverse = 1.0 / total
    delta = weighed * inverse
    rows = (o * inverse).astype(BF16)
    grads = ((a - delta * b) * (inverse * SCALE)).astype(BF16)
    aux = [m + jnp.log2(total) * (1.0 / RATE), delta, jnp.zeros((6, 128), F32)]
    return jnp.concatenate([rows, grads], axis=0), jnp.concatenate(aux, axis=0)


def pack_state(state):
    return jnp.concatenate([*state[:3], jnp.zeros((5, 128), F32)], axis=0), jnp.concatenate(state[3:], axis=0)


def load_state(rows, blocks):
    return (*[rows[i:i + 1] for i in range(3)], *[blocks[HEAD * i:HEAD * i + HEAD] for i in range(3)])


def split(row):
    parts = []
    for _ in range(3):
        part = row.astype(BF16).astype(F32)
        parts.append(part)
        row = row - part
    return parts


def key_side(k, v):
    ones, none = jnp.full((3, 128), -1.0, F32), jnp.zeros((3, 128), F32)
    rest = jnp.zeros((10, 256), F32)
    minus = jnp.concatenate(
        [jnp.concatenate([ones, none], axis=1), jnp.concatenate([none, ones], axis=1), rest], axis=0).astype(BF16)
    return jnp.concatenate([spread(k, v), minus], axis=0)


def key_tile(right, qg, aux):
    both = dot(jnp.concatenate([qg, aux], axis=0).T, right)
    prob = jnp.exp2(both[:, :128] * RATE)
    change = (prob * both[:, 128:]).astype(BF16)
    return jnp.concatenate([dot(qg[:HEAD], change), dot(qg[HEAD:], prob.astype(BF16))], axis=0)


def of_head(ref, x, h):
    return ref[x, HEAD * h:HEAD * h + HEAD]


def kernel(cap, far, send_list, tile_list, last_list, count_ref, q_ref, k_ref, v_ref, w_ref, og_ref,
           out_ref, dq_ref, dk_ref, dv_ref, *scratch):
    col, recv, col_aux, recv_aux = scratch[:4], scratch[4:8], scratch[8:10], scratch[10:12]
    (send, relay, send_aux,
     right, left, self_rows, self_blocks, both_t, aux_t, aux_own, attn_own,
     outgoing, incoming, send_sem, recv_sem) = scratch[12:]
    coords = place()
    y, z, core, hd, device = coords
    own = (z * 2 + core) * BLK
    sems = Sems(send_sem, recv_sem)
    rings = [Ring(col[unit], coords, sems, 2) for unit in range(4)]
    crosses = [Cross(send.at[unit % 2], relay.at[unit], recv[unit], cap, coords, sems) for unit in range(4)]
    aux_rings = [Ring(col_aux[h], coords, sems, 1) for h in (0, 1)]
    aux_crosses = [Spray(send_aux.at[h], recv_aux[h], cap, coords, sems) for h in (0, 1)]
    partners = [device(y, z, core, (hd + hop) % NX) for hop in range(1, NX)]
    partner_sem = sems.take(NX - 1)
    count = count_ref[0]
    groups = far // UNROLL

    def each(body, low=0, high=BLK):
        def step(x, carry):
            body(x)
            return carry

        lax.fori_loop(low, high, step, 0)

    def between(groups, body, state, slots):
        number = len(slots)

        def stretch(index, state):
            for place_of, calls in enumerate(slots):
                def run_calls(calls=calls):
                    for call in calls:
                        call()

                if calls:
                    pl.when(index == place_of)(run_calls)
            return lax.fori_loop(index * groups // number, (index + 1) * groups // number, body, state)

        return lax.fori_loop(0, number, stretch, state)

    def fill_kv(x):
        for h in (0, 1):
            col[h][own + x] = jnp.concatenate([of_head(k_ref, x, h), of_head(v_ref, x, h)], axis=0)

    def fill_qg(x):
        g = dot_nt(w_ref[...], og_ref[x]).astype(BF16)
        for h in (0, 1):
            q_head, g_head = of_head(q_ref, x, h), g[HEAD * h:HEAD * h + HEAD]
            col[2 + h][own + x] = jnp.concatenate([q_head, g_head], axis=0)
            right[h, x] = spread(q_head, g_head)
            left[h, x] = key_side(of_head(k_ref, x, h), of_head(v_ref, x, h))

    def self_query(h, slots):
        def body(group, carry):
            for u in range(UNROLL):
                x = group * UNROLL + u
                state = query_tile(jnp.concatenate([of_head(k_ref, x, h), of_head(v_ref, x, h)], axis=0), right[h, x])
                self_rows[h, x], self_blocks[h, x] = pack_state(state)
                both_t[h, far + x], aux_t[h, far + x] = query_result(state)
            return carry

        between(BLK // UNROLL, body, 0, slots)

    def entry(t):
        value = tile_list[t]
        x = value // 1024
        before = tile_list[jnp.maximum(t - 1, 0)] // 1024
        return value % 1024, x, (t == 0) | (before != x)

    def far_query(h, slots):
        def body(group, state):
            tiles = []
            for u in range(UNROLL):
                row, x, _ = entry(group * UNROLL + u)
                tiles.append(query_tile(recv[h][row], right[h, x]))
            for u in range(UNROLL):
                t = group * UNROLL + u
                _, x, fresh = entry(t)
                base = load_state(self_rows[h, x], self_blocks[h, x])
                state = tuple(jnp.where(fresh, b, s) for b, s in zip(base, state))
                skip = jnp.where(t < count, 0.0, NEG).astype(F32)
                state = query_merge(state, tiles[u], skip)
                both_t[h, t], aux_t[h, t] = query_result(state)
            return state

        row, block = jnp.zeros((1, 128), F32), jnp.zeros((HEAD, 128), F32)
        between(groups, body, (row, row, row, block, block, block), slots)

    def finish_query(h):
        def body(x):
            t = last_list[x]
            stats, both = aux_t[h, t], both_t[h, t]
            aux = jnp.concatenate([*split(stats[0:1]), *split(stats[1:2]), jnp.zeros((10, 128), F32)], axis=0).astype(BF16)
            aux_own[h, x] = aux
            col_aux[h][own + x] = aux
            attn_own[x, HEAD * h:HEAD * h + HEAD] = both[:HEAD]
            dq_ref[x, HEAD * h:HEAD * h + HEAD] = both[HEAD:]

        each(body)
        aux_rings[h].start()

    def project(a):
        part = lax.dot_general(attn_own[a], w_ref[...], (((0,), (0,)), ((), ())), preferred_element_type=F32).astype(BF16)
        for x in range(NX):
            outgoing[x, a] = part[32 * x:32 * x + 32]

    def self_key(h, slots):
        def body(group, carry):
            for u in range(UNROLL):
                x = group * UNROLL + u
                terms = key_tile(left[h, x], col[2 + h][own + x], aux_own[h, x])
                self_blocks[h, x, :64] = terms
                both_t[h, far + x] = terms.astype(BF16)
            return carry

        between(BLK // UNROLL, body, 0, slots)

    def far_key(h, slots):
        def body(group, state):
            tiles = []
            for u in range(UNROLL):
                row, x, _ = entry(group * UNROLL + u)
                tiles.append(key_tile(left[h, x], recv[2 + h][row], recv_aux[h][row]))
            for u in range(UNROLL):
                t = group * UNROLL + u
                _, x, fresh = entry(t)
                use = jnp.where(t < count, 1.0, 0.0).astype(F32)
                state = jnp.where(fresh, self_blocks[h, x, :64], state) + tiles[u] * use
                both_t[h, t] = state.astype(BF16)
            return state

        between(groups, body, jnp.zeros((64, 128), F32), slots)

    def finish_key(h):
        def body(x):
            terms = both_t[h, last_list[x]]
            dk_ref[x, HEAD * h:HEAD * h + HEAD] = (terms[:HEAD].astype(F32) * SCALE).astype(BF16)
            dv_ref[x, HEAD * h:HEAD * h + HEAD] = terms[HEAD:]

        each(body)

    def land(unit):
        rings[unit].advance(3)
        rings[unit].arrive()
        crosses[unit].pack(col[unit], send_list)

    def land_aux(h):
        aux_rings[h].advance(3)
        aux_rings[h].arrive()
        aux_crosses[h].pack(col_aux[h], send_list)

    def came(cross):
        cross.arrive()
        cross.drain()

    def at(ring, step, piece=0):
        return lambda: ring.event(step, piece)

    r0, r1, r2, r3 = rings
    a0, a1 = aux_rings
    each(fill_kv)
    meet(r0.peers() + aux_crosses[0].peer + partners)
    r0.start()
    each(fill_qg)
    r0.advance(0)
    self_query(0, [[], [at(r0, 1, 0)]])
    self_query(1, [[at(r0, 1, 1)], [at(r0, 2, 0)]])
    r0.event(2, 1)
    r1.start()
    land(0)
    r1.advance(0)
    r1.event(1, 0)
    crosses[0].relay_on()
    r1.event(1, 1)
    r1.advance(2)
    r2.start()
    land(1)
    r2.event(0, 0)
    came(crosses[0])
    far_query(0, [[], [at(r2, 0, 1)], [at(r2, 1, 0), crosses[1].relay_on], [at(r2, 1, 1)]])
    finish_query(0)
    r2.event(2, 0)
    a0.event(0, 0)
    r2.event(2, 1)
    r3.start()
    a0.event(1, 0)
    land(2)
    r3.event(0, 0)
    came(crosses[1])
    far_query(1, [[at(a0, 2)], [at(r3, 0, 1)], [lambda: land_aux(0), at(r3, 1, 0)], [crosses[2].relay_on, at(r3, 1, 1)]])
    finish_query(1)
    r3.event(2, 0)
    a1.event(0, 0)
    r3.event(2, 1)
    a1.event(1, 0)
    a1.event(2, 0)
    r3.advance(3)
    land_aux(1)
    r3.arrive()
    crosses[3].pack(col[3], send_list)
    each(project)
    legs = []
    for hop in range(1, NX):
        leg = sems.copy(outgoing.at[(hd + hop) % NX], incoming.at[hop - 1], partners[hop - 1], partner_sem + hop - 1)
        leg.start()
        legs.append(leg)
    self_key(0, [[]])
    crosses[3].relay_on()
    came(crosses[2])
    came(aux_crosses[0])
    far_key(0, [[]])
    finish_key(0)
    self_key(1, [[]])
    for leg in legs:
        leg.wait()

    def total(a):
        value = outgoing[hd, a].astype(F32)
        for hop in range(NX - 1):
            value += incoming[hop, a].astype(F32)
        out_ref[a] = value.astype(BF16)

    each(total)
    came(aux_crosses[1])
    came(crosses[3])
    far_key(1, [[]])
    finish_key(1)
    for ring in rings + aux_rings:
        ring.drain()


def run(cap, far, number, send_list, tile_list, last_list, count, *arrays):
    smem = pl.BlockSpec(memory_space=pltpu.SMEM)
    vmem = pl.BlockSpec(memory_space=pltpu.VMEM)
    sem = pltpu.SemaphoreType.DMA
    half = jax.ShapeDtypeStruct((BLK, 64, 128), BF16)

    def rows(units, count):
        return pltpu.VMEM((units, count, 64, 128), BF16)

    def alone(count, height=64):
        return pltpu.VMEM((count, height, 128), BF16)

    def aux(count):
        return pltpu.VMEM((2, count, 16, 128), BF16)

    def stats(count):
        return pltpu.VMEM((2, count, 8, 128), F32)

    scratch = [
        *[alone(COLUMN)] * 4, *[alone(4 * cap)] * 4, *[alone(COLUMN, 16)] * 2, *[alone(4 * cap, 16)] * 2,
        rows(2, 3 * cap), rows(4, cap), aux(3 * cap),
        pltpu.VMEM((2, BLK, 64, 256), BF16), pltpu.VMEM((2, BLK, 80, 256), BF16),
        stats(BLK), pltpu.VMEM((2, BLK, 96, 128), F32),
        rows(2, far + BLK), stats(far + BLK),
        aux(BLK), pltpu.VMEM((BLK, 64, 128), BF16),
        pltpu.VMEM((NX, BLK, 32, 256), BF16), pltpu.VMEM((NX - 1, BLK, 32, 256), BF16),
        sem((200,)), sem((200,)),
    ]
    return pl.pallas_call(
        functools.partial(kernel, cap, far),
        out_shape=(jax.ShapeDtypeStruct((BLK, 32, 256), BF16), half, half, half),
        in_specs=[smem] * 4 + [vmem] * 5, out_specs=(vmem,) * 4, scratch_shapes=scratch,
        compiler_params=pltpu.CompilerParams(collective_id=number, has_side_effects=True, vmem_limit_bytes=VMEM_LIMIT),
        name="attention",
    )(send_list[:, :cap].reshape(-1), tile_list[:far], last_list, count, *arrays)


def before(marks):
    rows, length = marks.shape
    cut = marks.astype(BF16).reshape(rows, length // 128, 128)
    lower = (jnp.arange(128)[:, None] < jnp.arange(128)[None, :]).astype(BF16)
    inside = jnp.einsum("rsc,cd->rsd", cut, lower, preferred_element_type=F32)
    sums = jnp.sum(cut.astype(F32), axis=2)
    ahead = jnp.arange(length // 128)[:, None] < jnp.arange(length // 128)[None, :]
    starts = jnp.sum(jnp.where(ahead[None], sums[:, :, None], 0.0), axis=1)
    return (inside + starts[:, :, None]).astype(jnp.int32).reshape(rows, length), jnp.sum(sums, axis=1).astype(jnp.int32)


def lists(pair_list, cap, far):
    me = lax.axis_index("blk")
    y, rest = me // (2 * NZ), me % (2 * NZ)
    near = jnp.concatenate([pair_list[0], pair_list[1]])
    away = jnp.concatenate([pair_list[1], pair_list[0]])
    near_dev, away_col = near // BLK, away // COLUMN
    hops = jnp.arange(NY, dtype=jnp.int32)
    asked = (near_dev[None] == ((y + hops) % NY * 2 * NZ + rest)[:, None]) & (away_col == y)[None]
    mine = near_dev == me
    source = mine[None] & (away_col[None] == ((y + hops) % NY)[:, None])
    at_block = mine[None] & ((near % BLK)[None] == jnp.arange(BLK, dtype=jnp.int32)[:, None])
    rank, sums = before(jnp.concatenate([asked, source, at_block], axis=0))
    place_of = jnp.arange(cap, dtype=jnp.int32)
    hit = asked[:, None] & (rank[:NY, None] == place_of[None, :, None])
    send_list = jnp.sum(jnp.where(hit, (away % COLUMN)[None, None], 0), axis=2)
    row = jnp.sum(jnp.where(source, rank[NY:2 * NY] + hops[:, None] * cap, 0), axis=0)
    counts = sums[2 * NY:]
    starts = jnp.sum(jnp.where(jnp.arange(BLK)[None, :] < jnp.arange(BLK)[:, None], counts[None, :], 0), axis=1)
    spot = jnp.sum(jnp.where(at_block, rank[2 * NY:] + starts[:, None], 0), axis=0)
    spot = jnp.where(mine, spot, far)
    value = near % BLK * 1024 + row
    chosen = spot[None] == jnp.arange(far, dtype=jnp.int32)[:, None]
    tile_list = jnp.sum(jnp.where(chosen, value[None], 0), axis=1)
    count = jnp.sum(counts)
    tile_list = jnp.where(jnp.arange(far) < count, tile_list, (BLK - 1) * 1024)
    last_list = jnp.where(counts > 0, starts + counts - 1, far + jnp.arange(BLK))
    i32 = jnp.int32
    return send_list.astype(i32), tile_list.astype(i32), last_list.astype(i32), count[None].astype(i32)


def most(pair_list):
    near = jnp.concatenate([pair_list[0], pair_list[1]]) // BLK
    away = jnp.concatenate([pair_list[1], pair_list[0]]) // COLUMN
    bins = jnp.arange(64 * NY, dtype=jnp.int32)
    counts = jnp.sum(((near * NY + away)[None] == bins[:, None]).astype(jnp.int32), axis=1)
    return jnp.max(counts), jnp.max(jnp.sum(counts.reshape(64, NY), axis=1))


def deliver(*refs):
    copies = [pltpu.make_async_copy(refs[i], refs[4 + i], refs[8].at[i]) for i in range(4)]
    for copy in copies:
        copy.start()
    for copy in copies:
        copy.wait()


def local(queries, keys, values, out_weight, out_grad, pair_list):
    arrays = (queries, keys, values, out_weight, out_grad)

    def branch(cap, far, number):
        return lambda: run(cap, far, number, *lists(pair_list, cap, far), *arrays)

    rows, tiles = most(pair_list)
    results = lax.cond((rows <= 30) & (tiles <= 88), branch(30, 88, 0), branch(64, 160, 1))
    anywhere = pl.BlockSpec(memory_space=pl.ANY)
    return pl.pallas_call(
        deliver, out_shape=[jax.ShapeDtypeStruct(item.shape, item.dtype) for item in results],
        in_specs=[anywhere] * 4, out_specs=[anywhere] * 4, scratch_shapes=[pltpu.SemaphoreType.DMA((4,))], name="deliver")(*results)


def solution(mesh):
    blocks, weight = P("blk", "hd", None), P("hd", None)
    return jax.shard_map(
        local, mesh=mesh,
        in_specs=(blocks, blocks, blocks, weight, P("blk", None, None), P()),
        out_specs=(blocks,) * 4, check_vma=False)
```

```python
import functools

import jax
import jax.numpy as jnp
from jax import lax
from jax.experimental import pallas as pl
from jax.experimental.pallas import tpu as pltpu
from jax.sharding import PartitionSpec as P

MESH = pl.DeviceIdType.MESH
HEAD = 32
NY, NZ, NX = 4, 8, 4
BLK = 16
COLUMN = 2 * NZ * BLK
UNROLL = 8
NEG = -1e30
RATE = HEAD**-0.5 * 1.4426950408889634
SCALE = HEAD**-0.5
F32 = jnp.float32
BF16 = jnp.bfloat16
VMEM_LIMIT = 61 * 2**20


def place():
    blk, hd = lax.axis_index("blk"), lax.axis_index("hd")
    core, z, y = blk % 2, (blk // 2) % NZ, blk // (2 * NZ)

    def device(yy, zz, cc, xx):
        return ((yy * NZ + zz) * 2 + cc, xx)

    return y, z, core, hd, device


def meet(peers):
    barrier = pltpu.get_barrier_semaphore()
    for peer in peers:
        pl.semaphore_signal(barrier, inc=1, device_id=peer, device_id_type=MESH)
    pl.semaphore_wait(barrier, len(peers))


class Sems:
    def __init__(self, send, recv):
        self.send, self.recv, self.used = send, recv, 0

    def take(self, count):
        self.used += count
        return self.used - count

    def copy(self, source, target, peer, sem):
        return pltpu.make_async_remote_copy(
            src_ref=source, dst_ref=target, send_sem=self.send.at[sem], recv_sem=self.recv.at[sem],
            device_id=peer, device_id_type=MESH)


class Ring:
    def __init__(self, buffer, coords, sems, pieces, height=1):
        self.buffer, self.sems, self.pieces, self.height = buffer, sems, pieces, height
        y, z, core, hd, device = coords
        self.z, self.core = z, core
        self.peer = (device(y, (z + 1) % NZ, core, hd), device(y, (z + NZ - 1) % NZ, core, hd))
        self.twin = device(y, z, 1 - core, hd)
        self.size = BLK // pieces
        self.leg_sem, self.twin_sem = sems.take(8 * pieces), sems.take(8 * pieces)

    def peers(self):
        return [*self.peer, self.twin]

    def rows(self, z, core, start, count):
        return self.buffer.at[pl.ds(((z * 2 + core) * BLK + start) * self.height, count * self.height)]

    def leg(self, piece, step, way, arriving):
        hop = step + 1 if arriving else step
        z = (self.z - hop + NZ) % NZ if way == 0 else (self.z + hop) % NZ
        start, count = piece * self.size, self.size
        if step == 3:
            count //= 2
            start += way * count
        rows = self.rows(z, self.core, start, count)
        return self.sems.copy(rows, rows, self.peer[way], self.leg_sem + (piece * 4 + step) * 2 + way)

    def pass_on(self, piece, hop, core):
        rows = self.rows((self.z + hop + NZ) % NZ, core, piece * self.size, self.size)
        return self.sems.copy(rows, rows, self.twin, self.twin_sem + piece * 8 + hop % NZ)

    def start(self):
        for piece in range(self.pieces):
            for way in (0, 1):
                self.leg(piece, 0, way, False).start()
        for piece in range(self.pieces):
            self.pass_on(piece, 0, self.core).start()

    def event(self, step, piece):
        for way in (0, 1):
            self.leg(piece, step, way, True).wait_recv()
            if step < 3:
                self.leg(piece, step + 1, way, False).start()
                self.pass_on(piece, -1 - step if way == 0 else 1 + step, self.core).start()
        if step == 3:
            self.pass_on(piece, 4, self.core).start()

    def advance(self, step):
        for piece in range(self.pieces):
            self.event(step, piece)

    def arrive(self):
        for piece in range(self.pieces):
            for hop in range(NZ):
                self.pass_on(piece, hop, 1 - self.core).wait_recv()

    def drain(self):
        for piece in range(self.pieces):
            for step in range(4):
                for way in (0, 1):
                    self.leg(piece, step, way, False).wait_send()
            for hop in range(NZ):
                self.pass_on(piece, hop, self.core).wait_send()


def stride_of(cap):
    return (cap + 3) // 4 * 4


class Cross:
    def __init__(self, send, relay, recv, cap, coords, sems):
        self.send, self.relay, self.recv, self.cap, self.sems = send, relay, recv, cap, sems
        self.stride = stride_of(cap)
        y, z, core, hd, device = coords
        self.peer = (device((y + 1) % NY, z, core, hd), device((y + NY - 1) % NY, z, core, hd))
        self.sem = sems.take(6)

    def peers(self):
        return [*self.peer]

    def first(self, way):
        half = self.cap // 2
        return self.sems.copy(
            self.send.at[pl.ds(self.cap + way * half, half)], self.relay.at[pl.ds(way * half, half)], self.peer[way], self.sem + way)

    def second(self, way):
        half = self.cap // 2
        return self.sems.copy(
            self.relay.at[pl.ds(way * half, half)], self.recv.at[pl.ds(2 * self.stride + way * half, half)], self.peer[way],
            self.sem + 2 + way)

    def direct(self, way):
        return self.sems.copy(
            self.send.at[pl.ds(2 * way * self.cap, self.cap)],
            self.recv.at[pl.ds((3 - 2 * way) * self.stride, self.cap)], self.peer[way], self.sem + 4 + way)

    def move(self, column, list_ref, hop, target, base):
        def body(step, carry):
            for u in range(2):
                row = step * 2 + u
                target[base + row] = column[list_ref[hop * self.cap + row]]
            return carry

        lax.fori_loop(0, self.cap // 2, body, 0)

    def pack(self, column, list_ref):
        self.move(column, list_ref, 2, self.send, self.cap)
        for way in (0, 1):
            self.first(way).start()
        self.move(column, list_ref, 1, self.send, 0)
        self.direct(0).start()
        self.move(column, list_ref, 3, self.send, 2 * self.cap)
        self.direct(1).start()
        self.move(column, list_ref, 0, self.recv, 0)

    def relay_on(self):
        for way in (0, 1):
            self.first(way).wait_recv()
            self.second(way).start()

    def arrive(self):
        for way in (0, 1):
            self.direct(way).wait_recv()
            self.second(way).wait_recv()

    def drain(self):
        for way in (0, 1):
            self.first(way).wait_send()
            self.direct(way).wait_send()
            self.second(way).wait_send()


class Spray:
    def __init__(self, send, recv, cap, coords, sems):
        self.send, self.recv, self.cap, self.sems = send, recv, cap, sems
        self.rows = 2 * stride_of(cap)
        y, z, core, hd, device = coords
        self.peer = [device((y + hop) % NY, z, core, hd) for hop in range(1, NY)]
        self.sem = sems.take(NY - 1)

    def leg(self, hop):
        return self.sems.copy(
            self.send.at[pl.ds((hop - 1) * self.rows, self.rows)], self.recv.at[pl.ds((NY - hop) * self.rows, self.rows)],
            self.peer[hop - 1], self.sem + hop - 1)

    def move(self, column, list_ref, hop, target, base):
        def body(step, carry):
            for u in range(2):
                row = step * 2 + u
                target[pl.ds(base + 2 * row, 2)] = column[pl.ds(2 * list_ref[hop * self.cap + row], 2)]
            return carry

        lax.fori_loop(0, self.cap // 2, body, 0)

    def pack(self, column, list_ref):
        for hop in (2, 1, 3):
            self.move(column, list_ref, hop, self.send, (hop - 1) * self.rows)
            self.leg(hop).start()
        self.move(column, list_ref, 0, self.recv, 0)

    def arrive(self):
        for hop in range(1, NY):
            self.leg(hop).wait_recv()

    def drain(self):
        for hop in range(1, NY):
            self.leg(hop).wait_send()


def spread(first, second):
    zero = jnp.zeros_like(first)
    return jnp.concatenate([jnp.concatenate([first, zero], axis=1), jnp.concatenate([zero, second], axis=1)], axis=0)


def dot(a, b):
    return jnp.dot(a, b, preferred_element_type=F32)


def dot_nt(a, b):
    return lax.dot_general(a, b, (((1,), (1,)), ((), ())), preferred_element_type=F32)


def query_tile(kv, right):
    both = dot(kv.T, right)
    scores, prob_grad = both[:, :128], both[:, 128:]
    top = jnp.max(scores, axis=0, keepdims=True)
    expo = jnp.exp2((scores - top) * RATE)
    total = jnp.sum(expo, axis=0, keepdims=True)
    weighed = jnp.sum(expo * prob_grad, axis=0, keepdims=True)
    mean = weighed / total
    change = (expo * (prob_grad - mean)).astype(BF16)
    by_expo = dot(kv, expo.astype(BF16))
    by_change = dot(kv[:HEAD], change)
    b, o = by_expo[:HEAD], by_expo[HEAD:]
    return top, total, weighed, o, by_change + mean * b, b


def query_merge(old, new, skip):
    (m0, *acc), (m1, *add) = old, new
    m1 = m1 + skip
    m = jnp.maximum(m0, m1)
    w0, w1 = jnp.exp2((m0 - m) * RATE), jnp.exp2((m1 - m) * RATE)
    return (m, *[x * w0 + y * w1 for x, y in zip(acc, add)])


def query_result(state):
    m, total, weighed, o, a, b = state
    inverse = 1.0 / total
    delta = weighed * inverse
    rows = (o * inverse).astype(BF16)
    grads = ((a - delta * b) * (inverse * SCALE)).astype(BF16)
    aux = [m + jnp.log2(total) * (1.0 / RATE), delta, jnp.zeros((6, 128), F32)]
    return jnp.concatenate([rows, grads], axis=0), jnp.concatenate(aux, axis=0)


def pack_state(state):
    return jnp.concatenate([*state[:3], jnp.zeros((5, 128), F32)], axis=0), jnp.concatenate(state[3:], axis=0)


def load_state(rows, blocks):
    return (*[rows[i:i + 1] for i in range(3)], *[blocks[HEAD * i:HEAD * i + HEAD] for i in range(3)])


def split(rows):
    parts = []
    for _ in range(3):
        part = rows.astype(BF16).astype(F32)
        parts.append(part)
        rows = rows - part
    return jnp.concatenate([*parts, jnp.zeros((10, 128), F32)], axis=0).astype(BF16)


def key_side(k, v):
    ones, none = jnp.full((1, 128), -1.0, F32), jnp.zeros((1, 128), F32)
    pair = jnp.concatenate([jnp.concatenate([ones, none], axis=1), jnp.concatenate([none, ones], axis=1)], axis=0)
    minus = jnp.concatenate([pair, pair, pair, jnp.zeros((10, 256), F32)], axis=0).astype(BF16)
    return jnp.concatenate([spread(k, v), minus], axis=0)


def key_tile(right, qg, stats):
    both = dot(jnp.concatenate([qg, split(stats)], axis=0).T, right)
    prob = jnp.exp2(both[:, :128] * RATE)
    change = (prob * both[:, 128:]).astype(BF16)
    return jnp.concatenate([dot(qg[:HEAD], change), dot(qg[HEAD:], prob.astype(BF16))], axis=0)


def of_head(ref, x, h):
    return ref[x, HEAD * h:HEAD * h + HEAD]


def kernel(cap, far, send_list, tile_list, last_list, count_ref, q_ref, k_ref, v_ref, w_ref, og_ref,
           out_ref, dq_ref, dk_ref, dv_ref, *scratch):
    col, recv, col_aux, recv_aux = scratch[:4], scratch[4:8], scratch[8:10], scratch[10:12]
    (send, relay, send_aux,
     right, left, self_rows, self_blocks, both_t, aux_t, aux_own, attn_own,
     outgoing, incoming, send_sem, recv_sem) = scratch[12:]
    coords = place()
    y, z, core, hd, device = coords
    own = (z * 2 + core) * BLK
    sems = Sems(send_sem, recv_sem)
    rings = [Ring(col[unit], coords, sems, 2) for unit in range(4)]
    crosses = [Cross(send.at[unit % 2], relay.at[unit], recv[unit], cap, coords, sems) for unit in range(4)]
    aux_rings = [Ring(col_aux[h], coords, sems, 1, 2) for h in (0, 1)]
    aux_crosses = [Spray(send_aux.at[h], recv_aux[h], cap, coords, sems) for h in (0, 1)]
    partners = [device(y, z, core, (hd + hop) % NX) for hop in range(1, NX)]
    partner_sem = sems.take(NX - 1)
    count = count_ref[0]
    groups = far // UNROLL

    def each(body, low=0, high=BLK):
        def step(x, carry):
            body(x)
            return carry

        lax.fori_loop(low, high, step, 0)

    def between(groups, body, state, slots):
        number = len(slots)

        def stretch(index, state):
            for place_of, calls in enumerate(slots):
                def run_calls(calls=calls):
                    for call in calls:
                        call()

                if calls:
                    pl.when(index == place_of)(run_calls)
            return lax.fori_loop(index * groups // number, (index + 1) * groups // number, body, state)

        return lax.fori_loop(0, number, stretch, state)

    def fill_kv(x):
        for h in (0, 1):
            col[h][own + x] = jnp.concatenate([of_head(k_ref, x, h), of_head(v_ref, x, h)], axis=0)

    def fill_qg(x):
        g = dot_nt(w_ref[...], og_ref[x]).astype(BF16)
        for h in (0, 1):
            q_head, g_head = of_head(q_ref, x, h), g[HEAD * h:HEAD * h + HEAD]
            col[2 + h][own + x] = jnp.concatenate([q_head, g_head], axis=0)
            right[h, x] = spread(q_head, g_head)
            left[h, x] = key_side(of_head(k_ref, x, h), of_head(v_ref, x, h))

    def self_query(h, slots):
        def body(group, carry):
            for u in range(UNROLL):
                x = group * UNROLL + u
                state = query_tile(jnp.concatenate([of_head(k_ref, x, h), of_head(v_ref, x, h)], axis=0), right[h, x])
                self_rows[h, x], self_blocks[h, x] = pack_state(state)
                both_t[h, far + x], aux_t[h, far + x] = query_result(state)
            return carry

        between(BLK // UNROLL, body, 0, slots)

    def entry(t):
        value = tile_list[t]
        x = value // 1024
        before = tile_list[jnp.maximum(t - 1, 0)] // 1024
        return value % 1024, x, (t == 0) | (before != x)

    def far_query(h, slots):
        def body(group, state):
            tiles = []
            for u in range(UNROLL):
                row, x, _ = entry(group * UNROLL + u)
                tiles.append(query_tile(recv[h][row], right[h, x]))
            for u in range(UNROLL):
                t = group * UNROLL + u
                _, x, fresh = entry(t)
                base = load_state(self_rows[h, x], self_blocks[h, x])
                state = tuple(jnp.where(fresh, b, s) for b, s in zip(base, state))
                skip = jnp.where(t < count, 0.0, NEG).astype(F32)
                state = query_merge(state, tiles[u], skip)
                both_t[h, t], aux_t[h, t] = query_result(state)
            return state

        row, block = jnp.zeros((1, 128), F32), jnp.zeros((HEAD, 128), F32)
        between(groups, body, (row, row, row, block, block, block), slots)

    def finish_query(h):
        def body(x):
            t = last_list[x]
            stats, both = aux_t[h, t], both_t[h, t]
            aux_own[h, x] = stats
            col_aux[h][pl.ds((own + x) * 2, 2)] = stats[:2]
            attn_own[x, HEAD * h:HEAD * h + HEAD] = both[:HEAD]
            dq_ref[x, HEAD * h:HEAD * h + HEAD] = both[HEAD:]

        each(body)
        aux_rings[h].start()

    def project(a):
        part = lax.dot_general(attn_own[a], w_ref[...], (((0,), (0,)), ((), ())), preferred_element_type=F32).astype(BF16)
        for x in range(NX):
            outgoing[x, a] = part[32 * x:32 * x + 32]

    def self_key(h, slots):
        def body(group, carry):
            for u in range(UNROLL):
                x = group * UNROLL + u
                terms = key_tile(left[h, x], col[2 + h][own + x], aux_own[h, x][:2])
                self_blocks[h, x, :64] = terms
                both_t[h, far + x] = terms.astype(BF16)
            return carry

        between(BLK // UNROLL, body, 0, slots)

    def far_key(h, slots):
        def body(group, state):
            tiles = []
            for u in range(UNROLL):
                row, x, _ = entry(group * UNROLL + u)
                tiles.append(key_tile(left[h, x], recv[2 + h][row], recv_aux[h][pl.ds(2 * row, 2)]))
            for u in range(UNROLL):
                t = group * UNROLL + u
                _, x, fresh = entry(t)
                use = jnp.where(t < count, 1.0, 0.0).astype(F32)
                state = jnp.where(fresh, self_blocks[h, x, :64], state) + tiles[u] * use
                both_t[h, t] = state.astype(BF16)
            return state

        between(groups, body, jnp.zeros((64, 128), F32), slots)

    def finish_key(h):
        def body(x):
            terms = both_t[h, last_list[x]]
            dk_ref[x, HEAD * h:HEAD * h + HEAD] = (terms[:HEAD].astype(F32) * SCALE).astype(BF16)
            dv_ref[x, HEAD * h:HEAD * h + HEAD] = terms[HEAD:]

        each(body)

    def land(unit):
        rings[unit].advance(3)
        rings[unit].arrive()
        crosses[unit].pack(col[unit], send_list)

    def land_aux(h):
        aux_rings[h].advance(3)
        aux_rings[h].arrive()
        aux_crosses[h].pack(col_aux[h], send_list)

    def came(cross):
        cross.arrive()
        cross.drain()

    def at(ring, step, piece=0):
        return lambda: ring.event(step, piece)

    r0, r1, r2, r3 = rings
    a0, a1 = aux_rings
    each(fill_kv)
    meet(r0.peers() + aux_crosses[0].peer + partners)
    r0.start()
    each(fill_qg)
    r0.advance(0)
    self_query(0, [[], [at(r0, 1, 0)]])
    self_query(1, [[at(r0, 1, 1)], [at(r0, 2, 0)]])
    r0.event(2, 1)
    r1.start()
    land(0)
    r1.advance(0)
    r1.event(1, 0)
    crosses[0].relay_on()
    r1.event(1, 1)
    r1.advance(2)
    r2.start()
    land(1)
    r2.event(0, 0)
    came(crosses[0])
    far_query(0, [[], [at(r2, 0, 1)], [at(r2, 1, 0), crosses[1].relay_on], [at(r2, 1, 1)]])
    finish_query(0)
    r2.event(2, 0)
    a0.event(0, 0)
    r2.event(2, 1)
    r3.start()
    a0.event(1, 0)
    land(2)
    r3.event(0, 0)
    came(crosses[1])
    far_query(1, [[at(a0, 2)], [at(r3, 0, 1)], [lambda: land_aux(0), at(r3, 1, 0)], [crosses[2].relay_on, at(r3, 1, 1)]])
    finish_query(1)
    r3.event(2, 0)
    a1.event(0, 0)
    r3.event(2, 1)
    a1.event(1, 0)
    a1.event(2, 0)
    r3.advance(3)
    land_aux(1)
    r3.arrive()
    crosses[3].pack(col[3], send_list)
    each(project)
    legs = []
    for hop in range(1, NX):
        leg = sems.copy(outgoing.at[(hd + hop) % NX], incoming.at[hop - 1], partners[hop - 1], partner_sem + hop - 1)
        leg.start()
        legs.append(leg)
    self_key(0, [[]])
    crosses[3].relay_on()
    came(crosses[2])
    came(aux_crosses[0])
    far_key(0, [[]])
    finish_key(0)
    self_key(1, [[]])
    for leg in legs:
        leg.wait()

    def total(a):
        value = outgoing[hd, a].astype(F32)
        for hop in range(NX - 1):
            value += incoming[hop, a].astype(F32)
        out_ref[a] = value.astype(BF16)

    each(total)
    came(aux_crosses[1])
    came(crosses[3])
    far_key(1, [[]])
    finish_key(1)
    for ring in rings + aux_rings:
        ring.drain()


def run(cap, far, number, send_list, tile_list, last_list, count, *arrays):
    smem = pl.BlockSpec(memory_space=pltpu.SMEM)
    vmem = pl.BlockSpec(memory_space=pltpu.VMEM)
    sem = pltpu.SemaphoreType.DMA
    half = jax.ShapeDtypeStruct((BLK, 64, 128), BF16)

    def rows(units, count):
        return pltpu.VMEM((units, count, 64, 128), BF16)

    stride = stride_of(cap)

    def alone(count):
        return pltpu.VMEM((count, 64, 128), BF16)

    def flat(count):
        return pltpu.VMEM((count, 128), F32)

    def stats(count):
        return pltpu.VMEM((2, count, 8, 128), F32)

    scratch = [
        *[alone(COLUMN)] * 4, *[alone(4 * stride)] * 4, *[flat(2 * COLUMN)] * 2, *[flat(8 * stride)] * 2,
        rows(2, 3 * cap), rows(4, cap), pltpu.VMEM((2, 6 * stride, 128), F32),
        pltpu.VMEM((2, BLK, 64, 256), BF16), pltpu.VMEM((2, BLK, 80, 256), BF16),
        stats(BLK), pltpu.VMEM((2, BLK, 96, 128), F32),
        rows(2, far + BLK), stats(far + BLK),
        stats(BLK), pltpu.VMEM((BLK, 64, 128), BF16),
        pltpu.VMEM((NX, BLK, 32, 256), BF16), pltpu.VMEM((NX - 1, BLK, 32, 256), BF16),
        sem((200,)), sem((200,)),
    ]
    return pl.pallas_call(
        functools.partial(kernel, cap, far),
        out_shape=(jax.ShapeDtypeStruct((BLK, 32, 256), BF16), half, half, half),
        in_specs=[smem] * 4 + [vmem] * 5, out_specs=(vmem,) * 4, scratch_shapes=scratch,
        compiler_params=pltpu.CompilerParams(collective_id=number, has_side_effects=True, vmem_limit_bytes=VMEM_LIMIT),
        name="attention",
    )(send_list, tile_list, last_list, count, *arrays)


def before(marks):
    rows, length = marks.shape
    cut = marks.astype(BF16).reshape(rows, length // 128, 128)
    lower = (jnp.arange(128)[:, None] < jnp.arange(128)[None, :]).astype(BF16)
    inside = jnp.einsum("rsc,cd->rsd", cut, lower, preferred_element_type=F32)
    sums = jnp.sum(cut.astype(F32), axis=2)
    ahead = jnp.arange(length // 128)[:, None] < jnp.arange(length // 128)[None, :]
    starts = jnp.sum(jnp.where(ahead[None], sums[:, :, None], 0.0), axis=1)
    return (inside + starts[:, :, None]).astype(jnp.int32).reshape(rows, length), jnp.sum(sums, axis=1).astype(jnp.int32)


def lists(pair_list, cap, far):
    me = lax.axis_index("blk")
    y, rest = me // (2 * NZ), me % (2 * NZ)
    near = jnp.concatenate([pair_list[0], pair_list[1]])
    away = jnp.concatenate([pair_list[1], pair_list[0]])
    near_dev, away_col = near // BLK, away // COLUMN
    hops = jnp.arange(NY, dtype=jnp.int32)
    asked = (near_dev[None] == ((y + hops) % NY * 2 * NZ + rest)[:, None]) & (away_col == y)[None]
    mine = near_dev == me
    source = mine[None] & (away_col[None] == ((y + hops) % NY)[:, None])
    at_block = mine[None] & ((near % BLK)[None] == jnp.arange(BLK, dtype=jnp.int32)[:, None])
    rank, sums = before(jnp.concatenate([asked, source, at_block], axis=0))
    row = jnp.sum(jnp.where(source, rank[NY:2 * NY] + hops[:, None] * stride_of(cap), 0), axis=0)
    counts = sums[2 * NY:]
    starts = jnp.sum(jnp.where(jnp.arange(BLK)[None, :] < jnp.arange(BLK)[:, None], counts[None, :], 0), axis=1)
    spot = jnp.sum(jnp.where(at_block, rank[2 * NY:] + starts[:, None], 0), axis=0)
    spot = jnp.where(mine, spot, -1)
    sent_at = jnp.sum(jnp.where(asked, rank[:NY] + hops[:, None] * cap + 1, 0), axis=0) - 1
    length = max(far, NY * cap)
    chosen = jnp.stack([sent_at, spot])[:, None, :] == jnp.arange(length, dtype=jnp.int32)[None, :, None]
    value = jnp.stack([away % COLUMN, near % BLK * 1024 + row])
    both = jnp.sum(jnp.where(chosen, value[:, None, :], 0), axis=2)
    count = jnp.sum(counts)
    send_list = both[0]
    tile_list = jnp.where(jnp.arange(length) < count, both[1], (BLK - 1) * 1024)
    last_list = jnp.where(counts > 0, starts + counts - 1, far + jnp.arange(BLK))
    i32 = jnp.int32
    return send_list.astype(i32), tile_list.astype(i32), last_list.astype(i32), count[None].astype(i32)


def fits(pair_list, cap, far):
    near = jnp.concatenate([pair_list[0], pair_list[1]]) // BLK
    away = jnp.concatenate([pair_list[1], pair_list[0]]) // COLUMN
    kinds = jnp.arange(NY + 1, dtype=jnp.int32)
    devices = jnp.arange(2 * NY * NZ, dtype=jnp.int32)
    found = (near[None, None] == devices[:, None, None]) & ((away[None, None] == kinds[None, :, None]) | (kinds == NY)[None, :, None])
    counts = jnp.sum(found.astype(jnp.int32), axis=2)
    limits = jnp.where(kinds == NY, far, cap)
    return jnp.max(counts - limits[None]) <= 0


def deliver(*refs):
    copies = [pltpu.make_async_copy(refs[i], refs[4 + i], refs[8].at[i]) for i in range(4)]
    for copy in copies:
        copy.start()
    for copy in copies:
        copy.wait()


def local(queries, keys, values, out_weight, out_grad, pair_list):
    arrays = (queries, keys, values, out_weight, out_grad)

    def branch(cap, far, number):
        return lambda: run(cap, far, number, *lists(pair_list, cap, far), *arrays)

    results = lax.cond(fits(pair_list, 30, 88), branch(30, 88, 0), branch(64, 160, 1))
    anywhere = pl.BlockSpec(memory_space=pl.ANY)
    return pl.pallas_call(
        deliver, out_shape=[jax.ShapeDtypeStruct(item.shape, item.dtype) for item in results],
        in_specs=[anywhere] * 4, out_specs=[anywhere] * 4, scratch_shapes=[pltpu.SemaphoreType.DMA((4,))], name="deliver")(*results)


def solution(mesh):
    blocks, weight = P("blk", "hd", None), P("hd", None)
    return jax.shard_map(
        local, mesh=mesh,
        in_specs=(blocks, blocks, blocks, weight, P("blk", None, None), P()),
        out_specs=(blocks,) * 4, check_vma=False)
```

```python
import functools

import jax
import jax.numpy as jnp
from jax import lax
from jax.experimental import pallas as pl
from jax.experimental.pallas import tpu as pltpu
from jax.sharding import PartitionSpec as P

MESH = pl.DeviceIdType.MESH
HEAD = 32
NY, NZ, NX = 4, 8, 4
BLK = 16
COLUMN = 2 * NZ * BLK
UNROLL = 8
NEG = -1e30
RATE = HEAD**-0.5 * 1.4426950408889634
SCALE = HEAD**-0.5
F32 = jnp.float32
BF16 = jnp.bfloat16
VMEM_LIMIT = 61 * 2**20


def place():
    blk, hd = lax.axis_index("blk"), lax.axis_index("hd")
    core, z, y = blk % 2, (blk // 2) % NZ, blk // (2 * NZ)

    def device(yy, zz, cc, xx):
        return ((yy * NZ + zz) * 2 + cc, xx)

    return y, z, core, hd, device


def meet(peers):
    barrier = pltpu.get_barrier_semaphore()
    for peer in peers:
        pl.semaphore_signal(barrier, inc=1, device_id=peer, device_id_type=MESH)
    pl.semaphore_wait(barrier, len(peers))


class Sems:
    def __init__(self, send, recv):
        self.send, self.recv, self.used = send, recv, 0

    def take(self, count):
        self.used += count
        return self.used - count

    def copy(self, source, target, peer, sem):
        return pltpu.make_async_remote_copy(
            src_ref=source, dst_ref=target, send_sem=self.send.at[sem], recv_sem=self.recv.at[sem],
            device_id=peer, device_id_type=MESH)


class Ring:
    def __init__(self, buffer, coords, sems, pieces, height=1):
        self.buffer, self.sems, self.pieces, self.height = buffer, sems, pieces, height
        y, z, core, hd, device = coords
        self.z, self.core = z, core
        self.peer = (device(y, (z + 1) % NZ, core, hd), device(y, (z + NZ - 1) % NZ, core, hd))
        self.twin = device(y, z, 1 - core, hd)
        self.size = BLK // pieces
        self.leg_sem, self.twin_sem = sems.take(8 * pieces), sems.take(8 * pieces)

    def peers(self):
        return [*self.peer, self.twin]

    def rows(self, z, core, start, count):
        return self.buffer.at[pl.ds(((z * 2 + core) * BLK + start) * self.height, count * self.height)]

    def leg(self, piece, step, way, arriving):
        hop = step + 1 if arriving else step
        z = (self.z - hop + NZ) % NZ if way == 0 else (self.z + hop) % NZ
        start, count = piece * self.size, self.size
        if step == 3:
            count //= 2
            start += way * count
        rows = self.rows(z, self.core, start, count)
        return self.sems.copy(rows, rows, self.peer[way], self.leg_sem + (piece * 4 + step) * 2 + way)

    def pass_on(self, piece, hop, core):
        rows = self.rows((self.z + hop + NZ) % NZ, core, piece * self.size, self.size)
        return self.sems.copy(rows, rows, self.twin, self.twin_sem + piece * 8 + hop % NZ)

    def start(self):
        for piece in range(self.pieces):
            for way in (0, 1):
                self.leg(piece, 0, way, False).start()
        for piece in range(self.pieces):
            self.pass_on(piece, 0, self.core).start()

    def event(self, step, piece):
        for way in (0, 1):
            self.leg(piece, step, way, True).wait_recv()
            if step < 3:
                self.leg(piece, step + 1, way, False).start()
                self.pass_on(piece, -1 - step if way == 0 else 1 + step, self.core).start()
        if step == 3:
            self.pass_on(piece, 4, self.core).start()

    def advance(self, step):
        for piece in range(self.pieces):
            self.event(step, piece)

    def arrive(self):
        for piece in range(self.pieces):
            for hop in range(NZ):
                self.pass_on(piece, hop, 1 - self.core).wait_recv()

    def drain(self):
        for piece in range(self.pieces):
            for step in range(4):
                for way in (0, 1):
                    self.leg(piece, step, way, False).wait_send()
            for hop in range(NZ):
                self.pass_on(piece, hop, self.core).wait_send()


def stride_of(cap):
    return (cap + 3) // 4 * 4


class Cross:
    def __init__(self, send, relay, recv, cap, coords, sems):
        self.send, self.relay, self.recv, self.cap, self.sems = send, relay, recv, cap, sems
        self.stride = stride_of(cap)
        y, z, core, hd, device = coords
        self.peer = (device((y + 1) % NY, z, core, hd), device((y + NY - 1) % NY, z, core, hd))
        self.sem = sems.take(6)

    def peers(self):
        return [*self.peer]

    def first(self, way):
        half = self.cap // 2
        return self.sems.copy(
            self.send.at[pl.ds(self.cap + way * half, half)], self.relay.at[pl.ds(way * half, half)], self.peer[way], self.sem + way)

    def second(self, way):
        half = self.cap // 2
        return self.sems.copy(
            self.relay.at[pl.ds(way * half, half)], self.recv.at[pl.ds(2 * self.stride + way * half, half)], self.peer[way],
            self.sem + 2 + way)

    def direct(self, way):
        return self.sems.copy(
            self.send.at[pl.ds(2 * way * self.cap, self.cap)],
            self.recv.at[pl.ds((3 - 2 * way) * self.stride, self.cap)], self.peer[way], self.sem + 4 + way)

    def move(self, column, list_ref, hop, target, base):
        def body(step, carry):
            for u in range(2):
                row = step * 2 + u
                target[base + row] = column[list_ref[hop * self.cap + row]]
            return carry

        lax.fori_loop(0, self.cap // 2, body, 0)

    def pack(self, column, list_ref):
        self.move(column, list_ref, 2, self.send, self.cap)
        for way in (0, 1):
            self.first(way).start()
        self.move(column, list_ref, 1, self.send, 0)
        self.direct(0).start()
        self.move(column, list_ref, 3, self.send, 2 * self.cap)
        self.direct(1).start()
        self.move(column, list_ref, 0, self.recv, 0)

    def relay_on(self):
        for way in (0, 1):
            self.first(way).wait_recv()
            self.second(way).start()

    def arrive(self):
        for way in (0, 1):
            self.direct(way).wait_recv()
            self.second(way).wait_recv()

    def drain(self):
        for way in (0, 1):
            self.first(way).wait_send()
            self.direct(way).wait_send()
            self.second(way).wait_send()


class Spray:
    def __init__(self, send, recv, cap, coords, sems):
        self.send, self.recv, self.cap, self.sems = send, recv, cap, sems
        self.rows = 2 * stride_of(cap)
        y, z, core, hd, device = coords
        self.peer = [device((y + hop) % NY, z, core, hd) for hop in range(1, NY)]
        self.sem = sems.take(NY - 1)

    def leg(self, hop):
        return self.sems.copy(
            self.send.at[pl.ds((hop - 1) * self.rows, self.rows)], self.recv.at[pl.ds((NY - hop) * self.rows, self.rows)],
            self.peer[hop - 1], self.sem + hop - 1)

    def move(self, column, list_ref, hop, target, base):
        def body(step, carry):
            for u in range(2):
                row = step * 2 + u
                target[pl.ds(base + 2 * row, 2)] = column[pl.ds(2 * list_ref[hop * self.cap + row], 2)]
            return carry

        lax.fori_loop(0, self.cap // 2, body, 0)

    def pack(self, column, list_ref):
        for hop in (2, 1, 3):
            self.move(column, list_ref, hop, self.send, (hop - 1) * self.rows)
            self.leg(hop).start()
        self.move(column, list_ref, 0, self.recv, 0)

    def arrive(self):
        for hop in range(1, NY):
            self.leg(hop).wait_recv()

    def drain(self):
        for hop in range(1, NY):
            self.leg(hop).wait_send()


def spread(first, second):
    zero = jnp.zeros_like(first)
    return jnp.concatenate([jnp.concatenate([first, zero], axis=1), jnp.concatenate([zero, second], axis=1)], axis=0)


def dot(a, b):
    return jnp.dot(a, b, preferred_element_type=F32)


def dot_nt(a, b):
    return lax.dot_general(a, b, (((1,), (1,)), ((), ())), preferred_element_type=F32)


def query_tile(kv, right):
    both = dot(kv.T, right)
    scores, prob_grad = both[:, :128], both[:, 128:]
    top = jnp.max(scores, axis=0, keepdims=True)
    expo = jnp.exp2((scores - top) * RATE)
    total = jnp.sum(expo, axis=0, keepdims=True)
    weighed = jnp.sum(expo * prob_grad, axis=0, keepdims=True)
    mean = weighed / total
    change = (expo * (prob_grad - mean)).astype(BF16)
    by_expo = dot(kv, expo.astype(BF16))
    by_change = dot(kv[:HEAD], change)
    b, o = by_expo[:HEAD], by_expo[HEAD:]
    return top, total, weighed, o, by_change + mean * b, b


def query_merge(old, new, skip):
    (m0, *acc), (m1, *add) = old, new
    m1 = m1 + skip
    m = jnp.maximum(m0, m1)
    w0, w1 = jnp.exp2((m0 - m) * RATE), jnp.exp2((m1 - m) * RATE)
    return (m, *[x * w0 + y * w1 for x, y in zip(acc, add)])


def query_result(state):
    m, total, weighed, o, a, b = state
    inverse = 1.0 / total
    delta = weighed * inverse
    rows = (o * inverse).astype(BF16)
    grads = ((a - delta * b) * (inverse * SCALE)).astype(BF16)
    aux = [m + jnp.log2(total) * (1.0 / RATE), delta, jnp.zeros((6, 128), F32)]
    return jnp.concatenate([rows, grads], axis=0), jnp.concatenate(aux, axis=0)


def pack_state(state):
    return jnp.concatenate([*state[:3], jnp.zeros((5, 128), F32)], axis=0), jnp.concatenate(state[3:], axis=0)


def load_state(rows, blocks):
    return (*[rows[i:i + 1] for i in range(3)], *[blocks[HEAD * i:HEAD * i + HEAD] for i in range(3)])


def split(rows):
    parts = []
    for _ in range(3):
        part = rows.astype(BF16).astype(F32)
        parts.append(part)
        rows = rows - part
    return jnp.concatenate([*parts, jnp.zeros((10, 128), F32)], axis=0).astype(BF16)


def key_side(k, v):
    ones, none = jnp.full((1, 128), -1.0, F32), jnp.zeros((1, 128), F32)
    pair = jnp.concatenate([jnp.concatenate([ones, none], axis=1), jnp.concatenate([none, ones], axis=1)], axis=0)
    minus = jnp.concatenate([pair, pair, pair, jnp.zeros((10, 256), F32)], axis=0).astype(BF16)
    return jnp.concatenate([spread(k, v), minus], axis=0)


def key_tile(right, qg, stats):
    both = dot(jnp.concatenate([qg, split(stats)], axis=0).T, right)
    prob = jnp.exp2(both[:, :128] * RATE)
    change = (prob * both[:, 128:]).astype(BF16)
    return jnp.concatenate([dot(qg[:HEAD], change), dot(qg[HEAD:], prob.astype(BF16))], axis=0)


def of_head(ref, x, h):
    return ref[x, HEAD * h:HEAD * h + HEAD]


def kernel(cap, far, send_list, tile_list, last_list, count_ref, q_ref, k_ref, v_ref, w_ref, og_far,
           out_ref, dq_ref, dk_ref, dv_ref, *scratch):
    col, recv, col_aux, recv_aux = scratch[:4], scratch[4:8], scratch[8:10], scratch[10:12]
    (send, relay, send_aux,
     right, left, self_rows, self_blocks, both_t, aux_t, aux_own, attn_own,
     outgoing, incoming, og_ref, og_sem, send_sem, recv_sem) = scratch[12:]
    og_copy = pltpu.make_async_copy(og_far, og_ref, og_sem)
    og_copy.start()
    coords = place()
    y, z, core, hd, device = coords
    own = (z * 2 + core) * BLK
    sems = Sems(send_sem, recv_sem)
    rings = [Ring(col[unit], coords, sems, 2) for unit in range(4)]
    crosses = [Cross(send.at[unit % 2], relay.at[unit], recv[unit], cap, coords, sems) for unit in range(4)]
    aux_rings = [Ring(col_aux[h], coords, sems, 1, 2) for h in (0, 1)]
    aux_crosses = [Spray(send_aux.at[h], recv_aux[h], cap, coords, sems) for h in (0, 1)]
    partners = [device(y, z, core, (hd + hop) % NX) for hop in range(1, NX)]
    partner_sem = sems.take(NX - 1)
    count = count_ref[0]
    groups = far // UNROLL

    def each(body, low=0, high=BLK):
        def step(x, carry):
            body(x)
            return carry

        lax.fori_loop(low, high, step, 0)

    def between(groups, body, state, slots):
        number = len(slots)

        def stretch(index, state):
            for place_of, calls in enumerate(slots):
                def run_calls(calls=calls):
                    for call in calls:
                        call()

                if calls:
                    pl.when(index == place_of)(run_calls)
            return lax.fori_loop(index * groups // number, (index + 1) * groups // number, body, state)

        return lax.fori_loop(0, number, stretch, state)

    def fill_kv(x):
        for h in (0, 1):
            col[h][own + x] = jnp.concatenate([of_head(k_ref, x, h), of_head(v_ref, x, h)], axis=0)

    def fill_qg(x):
        g = dot_nt(w_ref[...], og_ref[x]).astype(BF16)
        for h in (0, 1):
            q_head, g_head = of_head(q_ref, x, h), g[HEAD * h:HEAD * h + HEAD]
            col[2 + h][own + x] = jnp.concatenate([q_head, g_head], axis=0)
            right[h, x] = spread(q_head, g_head)
            left[h, x] = key_side(of_head(k_ref, x, h), of_head(v_ref, x, h))

    def self_query(h, slots):
        def body(group, carry):
            for u in range(UNROLL):
                x = group * UNROLL + u
                state = query_tile(jnp.concatenate([of_head(k_ref, x, h), of_head(v_ref, x, h)], axis=0), right[h, x])
                self_rows[h, x], self_blocks[h, x] = pack_state(state)
                both_t[h, far + x], aux_t[h, far + x] = query_result(state)
            return carry

        between(BLK // UNROLL, body, 0, slots)

    def entry(t):
        value = tile_list[t]
        x = value // 1024
        before = tile_list[jnp.maximum(t - 1, 0)] // 1024
        return value % 1024, x, (t == 0) | (before != x)

    def far_query(h, slots):
        def body(group, state):
            tiles = []
            for u in range(UNROLL):
                row, x, _ = entry(group * UNROLL + u)
                tiles.append(query_tile(recv[h][row], right[h, x]))
            for u in range(UNROLL):
                t = group * UNROLL + u
                _, x, fresh = entry(t)
                base = load_state(self_rows[h, x], self_blocks[h, x])
                state = tuple(jnp.where(fresh, b, s) for b, s in zip(base, state))
                skip = jnp.where(t < count, 0.0, NEG).astype(F32)
                state = query_merge(state, tiles[u], skip)
                both_t[h, t], aux_t[h, t] = query_result(state)
            return state

        row, block = jnp.zeros((1, 128), F32), jnp.zeros((HEAD, 128), F32)
        between(groups, body, (row, row, row, block, block, block), slots)

    def finish_query(h):
        def body(x):
            t = last_list[x]
            stats, both = aux_t[h, t], both_t[h, t]
            aux_own[h, x] = stats
            col_aux[h][pl.ds((own + x) * 2, 2)] = stats[:2]
            attn_own[x, HEAD * h:HEAD * h + HEAD] = both[:HEAD]
            dq_ref[x, HEAD * h:HEAD * h + HEAD] = both[HEAD:]

        each(body)
        aux_rings[h].start()

    def project(a):
        part = lax.dot_general(attn_own[a], w_ref[...], (((0,), (0,)), ((), ())), preferred_element_type=F32).astype(BF16)
        for x in range(NX):
            outgoing[x, a] = part[32 * x:32 * x + 32]

    def self_key(h, slots):
        def body(group, carry):
            for u in range(UNROLL):
                x = group * UNROLL + u
                terms = key_tile(left[h, x], col[2 + h][own + x], aux_own[h, x][:2])
                self_blocks[h, x, :64] = terms
                both_t[h, far + x] = terms.astype(BF16)
            return carry

        between(BLK // UNROLL, body, 0, slots)

    def far_key(h, slots):
        def body(group, state):
            tiles = []
            for u in range(UNROLL):
                row, x, _ = entry(group * UNROLL + u)
                tiles.append(key_tile(left[h, x], recv[2 + h][row], recv_aux[h][pl.ds(2 * row, 2)]))
            for u in range(UNROLL):
                t = group * UNROLL + u
                _, x, fresh = entry(t)
                use = jnp.where(t < count, 1.0, 0.0).astype(F32)
                state = jnp.where(fresh, self_blocks[h, x, :64], state) + tiles[u] * use
                both_t[h, t] = state.astype(BF16)
            return state

        between(groups, body, jnp.zeros((64, 128), F32), slots)

    def finish_key(h):
        def body(x):
            terms = both_t[h, last_list[x]]
            dk_ref[x, HEAD * h:HEAD * h + HEAD] = (terms[:HEAD].astype(F32) * SCALE).astype(BF16)
            dv_ref[x, HEAD * h:HEAD * h + HEAD] = terms[HEAD:]

        each(body)

    def land(unit):
        rings[unit].advance(3)
        rings[unit].arrive()
        crosses[unit].pack(col[unit], send_list)

    def land_aux(h):
        aux_rings[h].advance(3)
        aux_rings[h].arrive()
        aux_crosses[h].pack(col_aux[h], send_list)

    def came(cross):
        cross.arrive()
        cross.drain()

    def at(ring, step, piece=0):
        return lambda: ring.event(step, piece)

    r0, r1, r2, r3 = rings
    a0, a1 = aux_rings
    each(fill_kv)
    meet(r0.peers() + aux_crosses[0].peer + partners)
    r0.start()
    og_copy.wait()
    each(fill_qg)
    r0.advance(0)
    self_query(0, [[], [at(r0, 1, 0)]])
    self_query(1, [[at(r0, 1, 1)], [at(r0, 2, 0)]])
    r0.event(2, 1)
    r1.start()
    land(0)
    r1.advance(0)
    r1.event(1, 0)
    crosses[0].relay_on()
    r1.event(1, 1)
    r1.advance(2)
    r2.start()
    land(1)
    r2.event(0, 0)
    came(crosses[0])
    far_query(0, [[], [at(r2, 0, 1)], [at(r2, 1, 0), crosses[1].relay_on], [at(r2, 1, 1)]])
    finish_query(0)
    r2.event(2, 0)
    a0.event(0, 0)
    r2.event(2, 1)
    r3.start()
    a0.event(1, 0)
    land(2)
    r3.event(0, 0)
    came(crosses[1])
    far_query(1, [[at(a0, 2)], [at(r3, 0, 1)], [lambda: land_aux(0), at(r3, 1, 0)], [crosses[2].relay_on, at(r3, 1, 1)]])
    finish_query(1)
    r3.event(2, 0)
    a1.event(0, 0)
    r3.event(2, 1)
    a1.event(1, 0)
    a1.event(2, 0)
    r3.advance(3)
    land_aux(1)
    r3.arrive()
    crosses[3].pack(col[3], send_list)
    each(project)
    legs = []
    for hop in range(1, NX):
        leg = sems.copy(outgoing.at[(hd + hop) % NX], incoming.at[hop - 1], partners[hop - 1], partner_sem + hop - 1)
        leg.start()
        legs.append(leg)
    self_key(0, [[]])
    crosses[3].relay_on()
    came(crosses[2])
    came(aux_crosses[0])
    far_key(0, [[]])
    finish_key(0)
    self_key(1, [[]])
    for leg in legs:
        leg.wait()

    def total(a):
        value = outgoing[hd, a].astype(F32)
        for hop in range(NX - 1):
            value += incoming[hop, a].astype(F32)
        out_ref[a] = value.astype(BF16)

    each(total)
    came(aux_crosses[1])
    came(crosses[3])
    far_key(1, [[]])
    finish_key(1)
    for ring in rings + aux_rings:
        ring.drain()


def run(cap, far, number, send_list, tile_list, last_list, count, *arrays):
    smem = pl.BlockSpec(memory_space=pltpu.SMEM)
    vmem = pl.BlockSpec(memory_space=pltpu.VMEM)
    sem = pltpu.SemaphoreType.DMA
    half = jax.ShapeDtypeStruct((BLK, 64, 128), BF16)

    def rows(units, count):
        return pltpu.VMEM((units, count, 64, 128), BF16)

    stride = stride_of(cap)

    def alone(count):
        return pltpu.VMEM((count, 64, 128), BF16)

    def flat(count):
        return pltpu.VMEM((count, 128), F32)

    def stats(count):
        return pltpu.VMEM((2, count, 8, 128), F32)

    scratch = [
        *[alone(COLUMN)] * 4, *[alone(4 * stride)] * 4, *[flat(2 * COLUMN)] * 2, *[flat(8 * stride)] * 2,
        rows(2, 3 * cap), rows(4, cap), pltpu.VMEM((2, 6 * stride, 128), F32),
        pltpu.VMEM((2, BLK, 64, 256), BF16), pltpu.VMEM((2, BLK, 80, 256), BF16),
        stats(BLK), pltpu.VMEM((2, BLK, 96, 128), F32),
        rows(2, far + BLK), stats(far + BLK),
        stats(BLK), pltpu.VMEM((BLK, 64, 128), BF16),
        pltpu.VMEM((NX, BLK, 32, 256), BF16), pltpu.VMEM((NX - 1, BLK, 32, 256), BF16),
        pltpu.VMEM((BLK, 128, 256), BF16), sem, sem((200,)), sem((200,)),
    ]
    return pl.pallas_call(
        functools.partial(kernel, cap, far),
        out_shape=(jax.ShapeDtypeStruct((BLK, 32, 256), BF16), half, half, half),
        in_specs=[smem] * 4 + [vmem] * 4 + [pl.BlockSpec(memory_space=pl.ANY)], out_specs=(vmem,) * 4, scratch_shapes=scratch,
        compiler_params=pltpu.CompilerParams(collective_id=number, has_side_effects=True, vmem_limit_bytes=VMEM_LIMIT),
        name="attention",
    )(send_list, tile_list, last_list, count, *arrays)


def before(marks):
    rows, length = marks.shape
    cut = marks.astype(BF16).reshape(rows, length // 128, 128)
    lower = (jnp.arange(128)[:, None] < jnp.arange(128)[None, :]).astype(BF16)
    inside = jnp.einsum("rsc,cd->rsd", cut, lower, preferred_element_type=F32)
    sums = jnp.sum(cut.astype(F32), axis=2)
    ahead = jnp.arange(length // 128)[:, None] < jnp.arange(length // 128)[None, :]
    starts = jnp.sum(jnp.where(ahead[None], sums[:, :, None], 0.0), axis=1)
    return (inside + starts[:, :, None]).astype(jnp.int32).reshape(rows, length), jnp.sum(sums, axis=1).astype(jnp.int32)


def lists(near, away, cap, far):
    me = lax.axis_index("blk")
    y, rest = me // (2 * NZ), me % (2 * NZ)
    near_dev, away_col = near // BLK, away // COLUMN
    hops = jnp.arange(NY, dtype=jnp.int32)
    asked = (near_dev[None] == ((y + hops) % NY * 2 * NZ + rest)[:, None]) & (away_col == y)[None]
    mine = near_dev == me
    source = mine[None] & (away_col[None] == ((y + hops) % NY)[:, None])
    at_block = mine[None] & ((near % BLK)[None] == jnp.arange(BLK, dtype=jnp.int32)[:, None])
    rank, sums = before(jnp.concatenate([asked, source, at_block], axis=0))
    row = jnp.sum(jnp.where(source, rank[NY:2 * NY] + hops[:, None] * stride_of(cap), 0), axis=0)
    counts = sums[2 * NY:]
    starts = jnp.sum(jnp.where(jnp.arange(BLK)[None, :] < jnp.arange(BLK)[:, None], counts[None, :], 0), axis=1)
    spot = jnp.sum(jnp.where(at_block, rank[2 * NY:] + starts[:, None], 0), axis=0)
    spot = jnp.where(mine, spot, -1)
    sent_at = jnp.sum(jnp.where(asked, rank[:NY] + hops[:, None] * cap + 1, 0), axis=0) - 1
    length = max(far, NY * cap)
    chosen = jnp.stack([sent_at, spot])[:, None, :] == jnp.arange(length, dtype=jnp.int32)[None, :, None]
    value = jnp.stack([away % COLUMN, near % BLK * 1024 + row])
    both = jnp.sum(jnp.where(chosen, value[:, None, :], 0), axis=2)
    count = jnp.sum(counts)
    send_list = both[0]
    tile_list = jnp.where(jnp.arange(length) < count, both[1], (BLK - 1) * 1024)
    last_list = jnp.where(counts > 0, starts + counts - 1, far + jnp.arange(BLK))
    i32 = jnp.int32
    return send_list.astype(i32), tile_list.astype(i32), last_list.astype(i32), count[None].astype(i32)


def excess(near, away, cap, far):
    kinds = jnp.arange(NY + 1, dtype=jnp.int32)
    devices = jnp.arange(2 * NY * NZ, dtype=jnp.int32)
    by_kind = (away // COLUMN == kinds[:, None]) | (kinds == NY)[:, None]
    found = (near // BLK == devices[:, None])[:, None] & by_kind[None]
    counts = jnp.sum(found.astype(jnp.int32), axis=2)
    return jnp.max(jnp.where(kinds == NY, (counts - far) * 1000, counts - cap))


def deliver(*refs):
    copies = [pltpu.make_async_copy(refs[i], refs[4 + i], refs[8].at[i]) for i in range(4)]
    for copy in copies:
        copy.start()
    for copy in copies:
        copy.wait()


def local(queries, keys, values, out_weight, out_grad, pair_list):
    near = jnp.concatenate([pair_list[0], pair_list[1]])
    away = jnp.concatenate([pair_list[1], pair_list[0]])
    arrays = (queries, keys, values, out_weight, out_grad)

    def branch(cap, far, number):
        return lambda: run(cap, far, number, *lists(near, away, cap, far), *arrays)

    over = excess(near, away, 28, 88)
    index = (over > 0).astype(jnp.int32) + (over > 4).astype(jnp.int32)
    results = lax.switch(index, [branch(28, 88, 0), branch(32, 88, 1), branch(64, 160, 2)])
    anywhere = pl.BlockSpec(memory_space=pl.ANY)
    return pl.pallas_call(
        deliver, out_shape=[jax.ShapeDtypeStruct(item.shape, item.dtype) for item in results],
        in_specs=[anywhere] * 4, out_specs=[anywhere] * 4, scratch_shapes=[pltpu.SemaphoreType.DMA((4,))], name="deliver")(*results)


def solution(mesh):
    blocks, weight = P("blk", "hd", None), P("hd", None)
    return jax.shard_map(
        local, mesh=mesh,
        in_specs=(blocks, blocks, blocks, weight, P("blk", None, None), P()),
        out_specs=(blocks,) * 4, check_vma=False)
```

```python
import functools

import jax
import jax.numpy as jnp
from jax import lax
from jax.experimental import pallas as pl
from jax.experimental.pallas import tpu as pltpu
from jax.sharding import PartitionSpec as P

MESH = pl.DeviceIdType.MESH
HEAD = 32
NY, NZ, NX = 4, 8, 4
BLK = 16
COLUMN = 2 * NZ * BLK
UNROLL = 8
NEG = -1e30
RATE = HEAD**-0.5 * 1.4426950408889634
SCALE = HEAD**-0.5
F32 = jnp.float32
BF16 = jnp.bfloat16
VMEM_LIMIT = 61 * 2**20


def place():
    blk, hd = lax.axis_index("blk"), lax.axis_index("hd")
    core, z, y = blk % 2, (blk // 2) % NZ, blk // (2 * NZ)

    def device(yy, zz, cc, xx):
        return ((yy * NZ + zz) * 2 + cc, xx)

    return y, z, core, hd, device


def meet(peers):
    barrier = pltpu.get_barrier_semaphore()
    for peer in peers:
        pl.semaphore_signal(barrier, inc=1, device_id=peer, device_id_type=MESH)
    pl.semaphore_wait(barrier, len(peers))


class Sems:
    def __init__(self, send, recv):
        self.send, self.recv, self.used = send, recv, 0

    def take(self, count):
        self.used += count
        return self.used - count

    def copy(self, source, target, peer, sem):
        return pltpu.make_async_remote_copy(
            src_ref=source, dst_ref=target, send_sem=self.send.at[sem], recv_sem=self.recv.at[sem],
            device_id=peer, device_id_type=MESH)


class Ring:
    def __init__(self, buffer, coords, sems, pieces, height=1):
        self.buffer, self.sems, self.pieces, self.height = buffer, sems, pieces, height
        y, z, core, hd, device = coords
        self.z, self.core = z, core
        self.peer = (device(y, (z + 1) % NZ, core, hd), device(y, (z + NZ - 1) % NZ, core, hd))
        self.twin = device(y, z, 1 - core, hd)
        self.size = BLK // pieces
        self.leg_sem, self.twin_sem = sems.take(8 * pieces), sems.take(8 * pieces)

    def peers(self):
        return [*self.peer, self.twin]

    def rows(self, z, core, start, count):
        return self.buffer.at[pl.ds(((z * 2 + core) * BLK + start) * self.height, count * self.height)]

    def leg(self, piece, step, way, arriving):
        hop = step + 1 if arriving else step
        z = (self.z - hop + NZ) % NZ if way == 0 else (self.z + hop) % NZ
        start, count = piece * self.size, self.size
        if step == 3:
            count //= 2
            start += way * count
        rows = self.rows(z, self.core, start, count)
        return self.sems.copy(rows, rows, self.peer[way], self.leg_sem + (piece * 4 + step) * 2 + way)

    def pass_on(self, piece, hop, core):
        rows = self.rows((self.z + hop + NZ) % NZ, core, piece * self.size, self.size)
        return self.sems.copy(rows, rows, self.twin, self.twin_sem + piece * 8 + hop % NZ)

    def start(self):
        for piece in range(self.pieces):
            for way in (0, 1):
                self.leg(piece, 0, way, False).start()
        for piece in range(self.pieces):
            self.pass_on(piece, 0, self.core).start()

    def event(self, step, piece):
        for way in (0, 1):
            self.leg(piece, step, way, True).wait_recv()
            if step < 3:
                self.leg(piece, step + 1, way, False).start()
                self.pass_on(piece, -1 - step if way == 0 else 1 + step, self.core).start()
        if step == 3:
            self.pass_on(piece, 4, self.core).start()

    def advance(self, step):
        for piece in range(self.pieces):
            self.event(step, piece)

    def arrive(self):
        for piece in range(self.pieces):
            for hop in range(NZ):
                self.pass_on(piece, hop, 1 - self.core).wait_recv()

    def drain(self):
        for piece in range(self.pieces):
            for step in range(4):
                for way in (0, 1):
                    self.leg(piece, step, way, False).wait_send()
            for hop in range(NZ):
                self.pass_on(piece, hop, self.core).wait_send()


def stride_of(cap):
    return (cap + 3) // 4 * 4


class Cross:
    def __init__(self, send, relay, recv, cap, coords, sems):
        self.send, self.relay, self.recv, self.cap, self.sems = send, relay, recv, cap, sems
        self.stride = stride_of(cap)
        y, z, core, hd, device = coords
        self.peer = (device((y + 1) % NY, z, core, hd), device((y + NY - 1) % NY, z, core, hd))
        self.sem = sems.take(6)

    def peers(self):
        return [*self.peer]

    def first(self, way):
        half = self.cap // 2
        return self.sems.copy(
            self.send.at[pl.ds(self.cap + way * half, half)], self.relay.at[pl.ds(way * half, half)], self.peer[way], self.sem + way)

    def second(self, way):
        half = self.cap // 2
        return self.sems.copy(
            self.relay.at[pl.ds(way * half, half)], self.recv.at[pl.ds(2 * self.stride + way * half, half)], self.peer[way],
            self.sem + 2 + way)

    def direct(self, way):
        return self.sems.copy(
            self.send.at[pl.ds(2 * way * self.cap, self.cap)],
            self.recv.at[pl.ds((3 - 2 * way) * self.stride, self.cap)], self.peer[way], self.sem + 4 + way)

    def move(self, column, list_ref, hop, target, base):
        def body(step, carry):
            for u in range(2):
                row = step * 2 + u
                target[base + row] = column[list_ref[hop * self.cap + row]]
            return carry

        lax.fori_loop(0, self.cap // 2, body, 0)

    def pack(self, column, list_ref):
        self.move(column, list_ref, 2, self.send, self.cap)
        for way in (0, 1):
            self.first(way).start()
        self.move(column, list_ref, 1, self.send, 0)
        self.direct(0).start()
        self.move(column, list_ref, 3, self.send, 2 * self.cap)
        self.direct(1).start()
        self.move(column, list_ref, 0, self.recv, 0)

    def relay_on(self):
        for way in (0, 1):
            self.first(way).wait_recv()
            self.second(way).start()

    def arrive(self):
        for way in (0, 1):
            self.direct(way).wait_recv()
            self.second(way).wait_recv()

    def drain(self):
        for way in (0, 1):
            self.first(way).wait_send()
            self.direct(way).wait_send()
            self.second(way).wait_send()


class Spray:
    def __init__(self, send, recv, cap, coords, sems):
        self.send, self.recv, self.cap, self.sems = send, recv, cap, sems
        self.rows = 2 * stride_of(cap)
        y, z, core, hd, device = coords
        self.peer = [device((y + hop) % NY, z, core, hd) for hop in range(1, NY)]
        self.sem = sems.take(NY - 1)

    def leg(self, hop):
        return self.sems.copy(
            self.send.at[pl.ds((hop - 1) * self.rows, self.rows)], self.recv.at[pl.ds((NY - hop) * self.rows, self.rows)],
            self.peer[hop - 1], self.sem + hop - 1)

    def move(self, column, list_ref, hop, target, base):
        def body(step, carry):
            for u in range(2):
                row = step * 2 + u
                target[pl.ds(base + 2 * row, 2)] = column[pl.ds(2 * list_ref[hop * self.cap + row], 2)]
            return carry

        lax.fori_loop(0, self.cap // 2, body, 0)

    def pack(self, column, list_ref):
        for hop in (2, 1, 3):
            self.move(column, list_ref, hop, self.send, (hop - 1) * self.rows)
            self.leg(hop).start()
        self.move(column, list_ref, 0, self.recv, 0)

    def arrive(self):
        for hop in range(1, NY):
            self.leg(hop).wait_recv()

    def drain(self):
        for hop in range(1, NY):
            self.leg(hop).wait_send()


def spread(first, second):
    zero = jnp.zeros_like(first)
    return jnp.concatenate([jnp.concatenate([first, zero], axis=1), jnp.concatenate([zero, second], axis=1)], axis=0)


def dot(a, b):
    return jnp.dot(a, b, preferred_element_type=F32)


def dot_nt(a, b):
    return lax.dot_general(a, b, (((1,), (1,)), ((), ())), preferred_element_type=F32)


def query_tile(kv, right):
    both = dot(kv.T, right)
    scores, prob_grad = both[:, :128], both[:, 128:]
    top = jnp.max(scores, axis=0, keepdims=True)
    expo = jnp.exp2((scores - top) * RATE)
    total = jnp.sum(expo, axis=0, keepdims=True)
    weighed = jnp.sum(expo * prob_grad, axis=0, keepdims=True)
    mean = weighed / total
    change = (expo * (prob_grad - mean)).astype(BF16)
    by_expo = dot(kv, expo.astype(BF16))
    by_change = dot(kv[:HEAD], change)
    b, o = by_expo[:HEAD], by_expo[HEAD:]
    return top, total, weighed, o, by_change + mean * b, b


def query_merge(old, new, skip):
    (m0, *acc), (m1, *add) = old, new
    m1 = m1 + skip
    m = jnp.maximum(m0, m1)
    w0, w1 = jnp.exp2((m0 - m) * RATE), jnp.exp2((m1 - m) * RATE)
    return (m, *[x * w0 + y * w1 for x, y in zip(acc, add)])


def query_result(state):
    m, total, weighed, o, a, b = state
    inverse = 1.0 / total
    delta = weighed * inverse
    rows = (o * inverse).astype(BF16)
    grads = ((a - delta * b) * (inverse * SCALE)).astype(BF16)
    aux = [m + jnp.log2(total) * (1.0 / RATE), delta, jnp.zeros((6, 128), F32)]
    return jnp.concatenate([rows, grads], axis=0), jnp.concatenate(aux, axis=0)


def pack_state(state):
    return jnp.concatenate([*state[:3], jnp.zeros((5, 128), F32)], axis=0), jnp.concatenate(state[3:], axis=0)


def load_state(rows, blocks):
    return (*[rows[i:i + 1] for i in range(3)], *[blocks[HEAD * i:HEAD * i + HEAD] for i in range(3)])


def split(rows):
    parts = []
    for _ in range(3):
        part = rows.astype(BF16).astype(F32)
        parts.append(part)
        rows = rows - part
    return jnp.concatenate([*parts, jnp.zeros((10, 128), F32)], axis=0).astype(BF16)


def key_side(k, v):
    ones, none = jnp.full((1, 128), -1.0, F32), jnp.zeros((1, 128), F32)
    pair = jnp.concatenate([jnp.concatenate([ones, none], axis=1), jnp.concatenate([none, ones], axis=1)], axis=0)
    minus = jnp.concatenate([pair, pair, pair, jnp.zeros((10, 256), F32)], axis=0).astype(BF16)
    return jnp.concatenate([spread(k, v), minus], axis=0)


def key_tile(right, qg, stats):
    both = dot(jnp.concatenate([qg, split(stats)], axis=0).T, right)
    prob = jnp.exp2(both[:, :128] * RATE)
    change = (prob * both[:, 128:]).astype(BF16)
    return jnp.concatenate([dot(qg[:HEAD], change), dot(qg[HEAD:], prob.astype(BF16))], axis=0)


def of_head(ref, x, h):
    return ref[x, HEAD * h:HEAD * h + HEAD]


def kernel(cap, far, send_list, tile_list, last_list, count_ref, q_ref, k_ref, v_ref, w_ref, og_far,
           out_ref, dq_ref, dk_ref, dv_ref, *scratch):
    col, recv, col_aux, recv_aux = scratch[:4], scratch[4:8], scratch[8:10], scratch[10:12]
    (send, relay, send_aux,
     right, left, self_rows, self_blocks, both_t, aux_t, aux_own, attn_own,
     outgoing, incoming, og_ref, og_sem, send_sem, recv_sem) = scratch[12:]
    og_copy = pltpu.make_async_copy(og_far, og_ref, og_sem)
    og_copy.start()
    coords = place()
    y, z, core, hd, device = coords
    own = (z * 2 + core) * BLK
    sems = Sems(send_sem, recv_sem)
    rings = [Ring(col[unit], coords, sems, 2) for unit in range(4)]
    crosses = [Cross(send.at[unit % 2], relay.at[unit], recv[unit], cap, coords, sems) for unit in range(4)]
    aux_rings = [Ring(col_aux[h], coords, sems, 1, 2) for h in (0, 1)]
    aux_crosses = [Spray(send_aux.at[h], recv_aux[h], cap, coords, sems) for h in (0, 1)]
    partners = [device(y, z, core, (hd + hop) % NX) for hop in range(1, NX)]
    partner_sem = sems.take(NX - 1)
    count = count_ref[0]
    groups = far // UNROLL

    def each(body, low=0, high=BLK):
        def step(x, carry):
            body(x)
            return carry

        lax.fori_loop(low, high, step, 0)

    def between(groups, body, state, slots):
        number = len(slots)

        def stretch(index, state):
            for place_of, calls in enumerate(slots):
                def run_calls(calls=calls):
                    for call in calls:
                        call()

                if calls:
                    pl.when(index == place_of)(run_calls)
            return lax.fori_loop(index * groups // number, (index + 1) * groups // number, body, state)

        return lax.fori_loop(0, number, stretch, state)

    def fill_kv(x):
        for h in (0, 1):
            col[h][own + x] = jnp.concatenate([of_head(k_ref, x, h), of_head(v_ref, x, h)], axis=0)

    def fill_qg(x):
        g = dot_nt(w_ref[...], og_ref[x]).astype(BF16)
        for h in (0, 1):
            q_head, g_head = of_head(q_ref, x, h), g[HEAD * h:HEAD * h + HEAD]
            col[2 + h][own + x] = jnp.concatenate([q_head, g_head], axis=0)
            right[h, x] = spread(q_head, g_head)
            left[h, x] = key_side(of_head(k_ref, x, h), of_head(v_ref, x, h))

    def self_query(h, slots):
        def body(group, carry):
            for u in range(UNROLL):
                x = group * UNROLL + u
                state = query_tile(jnp.concatenate([of_head(k_ref, x, h), of_head(v_ref, x, h)], axis=0), right[h, x])
                self_rows[h, x], self_blocks[h, x] = pack_state(state)
                both_t[h, far + x], aux_t[h, far + x] = query_result(state)
            return carry

        between(BLK // UNROLL, body, 0, slots)

    def entry(t):
        value = tile_list[t]
        x = value // 1024
        before = tile_list[jnp.maximum(t - 1, 0)] // 1024
        return value % 1024, x, (t == 0) | (before != x)

    def far_query(h, slots):
        def body(group, state):
            tiles = []
            for u in range(UNROLL):
                row, x, _ = entry(group * UNROLL + u)
                tiles.append(query_tile(recv[h][row], right[h, x]))
            for u in range(UNROLL):
                t = group * UNROLL + u
                _, x, fresh = entry(t)
                base = load_state(self_rows[h, x], self_blocks[h, x])
                state = tuple(jnp.where(fresh, b, s) for b, s in zip(base, state))
                skip = jnp.where(t < count, 0.0, NEG).astype(F32)
                state = query_merge(state, tiles[u], skip)
                both_t[h, t], aux_t[h, t] = query_result(state)
            return state

        row, block = jnp.zeros((1, 128), F32), jnp.zeros((HEAD, 128), F32)
        between(groups, body, (row, row, row, block, block, block), slots)

    def finish_query(h):
        def body(x):
            t = last_list[x]
            stats, both = aux_t[h, t], both_t[h, t]
            aux_own[h, x] = stats
            col_aux[h][pl.ds((own + x) * 2, 2)] = stats[:2]
            attn_own[x, HEAD * h:HEAD * h + HEAD] = both[:HEAD]
            dq_ref[x, HEAD * h:HEAD * h + HEAD] = both[HEAD:]

        each(body)
        aux_rings[h].start()

    def project(a):
        part = lax.dot_general(attn_own[a], w_ref[...], (((0,), (0,)), ((), ())), preferred_element_type=F32).astype(BF16)
        for x in range(NX):
            outgoing[x, a] = part[32 * x:32 * x + 32]

    def self_key(h, slots):
        def body(group, carry):
            for u in range(UNROLL):
                x = group * UNROLL + u
                terms = key_tile(left[h, x], col[2 + h][own + x], aux_own[h, x][:2])
                self_blocks[h, x, :64] = terms
                both_t[h, far + x] = terms.astype(BF16)
            return carry

        between(BLK // UNROLL, body, 0, slots)

    def far_key(h, slots):
        def body(group, state):
            tiles = []
            for u in range(UNROLL):
                row, x, _ = entry(group * UNROLL + u)
                tiles.append(key_tile(left[h, x], recv[2 + h][row], recv_aux[h][pl.ds(2 * row, 2)]))
            for u in range(UNROLL):
                t = group * UNROLL + u
                _, x, fresh = entry(t)
                use = jnp.where(t < count, 1.0, 0.0).astype(F32)
                state = jnp.where(fresh, self_blocks[h, x, :64], state) + tiles[u] * use
                both_t[h, t] = state.astype(BF16)
            return state

        between(groups, body, jnp.zeros((64, 128), F32), slots)

    def finish_key(h):
        def body(x):
            terms = both_t[h, last_list[x]]
            dk_ref[x, HEAD * h:HEAD * h + HEAD] = (terms[:HEAD].astype(F32) * SCALE).astype(BF16)
            dv_ref[x, HEAD * h:HEAD * h + HEAD] = terms[HEAD:]

        each(body)

    def land(unit):
        rings[unit].advance(3)
        rings[unit].arrive()
        crosses[unit].pack(col[unit], send_list)

    def land_aux(h):
        aux_rings[h].advance(3)
        aux_rings[h].arrive()
        aux_crosses[h].pack(col_aux[h], send_list)

    def came(cross):
        cross.arrive()
        cross.drain()

    def at(ring, step, piece=0):
        return lambda: ring.event(step, piece)

    r0, r1, r2, r3 = rings
    a0, a1 = aux_rings
    each(fill_kv)
    meet(r0.peers() + aux_crosses[0].peer + partners)
    r0.start()
    og_copy.wait()
    each(fill_qg)
    r0.advance(0)
    self_query(0, [[], [at(r0, 1, 0)]])
    self_query(1, [[at(r0, 1, 1)], [at(r0, 2, 0)]])
    r0.event(2, 1)
    r1.start()
    land(0)
    r1.advance(0)
    r1.event(1, 0)
    crosses[0].relay_on()
    r1.event(1, 1)
    r1.advance(2)
    r2.start()
    land(1)
    r2.event(0, 0)
    came(crosses[0])
    far_query(0, [[], [at(r2, 0, 1)], [at(r2, 1, 0), crosses[1].relay_on], [at(r2, 1, 1)]])
    finish_query(0)
    r2.event(2, 0)
    a0.event(0, 0)
    r2.event(2, 1)
    r3.start()
    a0.event(1, 0)
    land(2)
    r3.event(0, 0)
    came(crosses[1])
    far_query(1, [[at(a0, 2)], [at(r3, 0, 1)], [lambda: land_aux(0), at(r3, 1, 0)], [crosses[2].relay_on, at(r3, 1, 1)]])
    finish_query(1)
    r3.event(2, 0)
    a1.event(0, 0)
    r3.event(2, 1)
    a1.event(1, 0)
    r3.advance(3)
    r3.arrive()
    crosses[3].pack(col[3], send_list)
    a1.event(2, 0)
    land_aux(1)
    each(project)
    legs = []
    for hop in range(1, NX):
        leg = sems.copy(outgoing.at[(hd + hop) % NX], incoming.at[hop - 1], partners[hop - 1], partner_sem + hop - 1)
        leg.start()
        legs.append(leg)
    self_key(0, [[]])
    crosses[3].relay_on()
    came(crosses[2])
    came(aux_crosses[0])
    far_key(0, [[]])
    finish_key(0)
    self_key(1, [[]])
    for leg in legs:
        leg.wait()

    def total(a):
        value = outgoing[hd, a].astype(F32)
        for hop in range(NX - 1):
            value += incoming[hop, a].astype(F32)
        out_ref[a] = value.astype(BF16)

    each(total)
    came(aux_crosses[1])
    came(crosses[3])
    far_key(1, [[]])
    finish_key(1)
    for ring in rings + aux_rings:
        ring.drain()


def run(cap, far, number, send_list, tile_list, last_list, count, *arrays):
    smem = pl.BlockSpec(memory_space=pltpu.SMEM)
    vmem = pl.BlockSpec(memory_space=pltpu.VMEM)
    sem = pltpu.SemaphoreType.DMA
    half = jax.ShapeDtypeStruct((BLK, 64, 128), BF16)

    def rows(units, count):
        return pltpu.VMEM((units, count, 64, 128), BF16)

    stride = stride_of(cap)

    def alone(count):
        return pltpu.VMEM((count, 64, 128), BF16)

    def flat(count):
        return pltpu.VMEM((count, 128), F32)

    def stats(count):
        return pltpu.VMEM((2, count, 8, 128), F32)

    scratch = [
        *[alone(COLUMN)] * 4, *[alone(4 * stride)] * 4, *[flat(2 * COLUMN)] * 2, *[flat(8 * stride)] * 2,
        rows(2, 3 * cap), rows(4, cap), pltpu.VMEM((2, 6 * stride, 128), F32),
        pltpu.VMEM((2, BLK, 64, 256), BF16), pltpu.VMEM((2, BLK, 80, 256), BF16),
        stats(BLK), pltpu.VMEM((2, BLK, 96, 128), F32),
        rows(2, far + BLK), stats(far + BLK),
        stats(BLK), pltpu.VMEM((BLK, 64, 128), BF16),
        pltpu.VMEM((NX, BLK, 32, 256), BF16), pltpu.VMEM((NX - 1, BLK, 32, 256), BF16),
        pltpu.VMEM((BLK, 128, 256), BF16), sem, sem((200,)), sem((200,)),
    ]
    return pl.pallas_call(
        functools.partial(kernel, cap, far),
        out_shape=(jax.ShapeDtypeStruct((BLK, 32, 256), BF16), half, half, half),
        in_specs=[smem] * 4 + [vmem] * 4 + [pl.BlockSpec(memory_space=pl.ANY)], out_specs=(vmem,) * 4, scratch_shapes=scratch,
        compiler_params=pltpu.CompilerParams(collective_id=number, has_side_effects=True, vmem_limit_bytes=VMEM_LIMIT),
        name="attention",
    )(send_list, tile_list, last_list, count, *arrays)


def before(marks):
    rows, length = marks.shape
    cut = marks.astype(BF16).reshape(rows, length // 128, 128)
    lower = (jnp.arange(128)[:, None] < jnp.arange(128)[None, :]).astype(BF16)
    inside = jnp.einsum("rsc,cd->rsd", cut, lower, preferred_element_type=F32)
    sums = jnp.sum(cut.astype(F32), axis=2)
    ahead = jnp.arange(length // 128)[:, None] < jnp.arange(length // 128)[None, :]
    starts = jnp.sum(jnp.where(ahead[None], sums[:, :, None], 0.0), axis=1)
    return (inside + starts[:, :, None]).astype(jnp.int32).reshape(rows, length), jnp.sum(sums, axis=1).astype(jnp.int32)


def lists(near, away, cap, far):
    me = lax.axis_index("blk")
    y, rest = me // (2 * NZ), me % (2 * NZ)
    near_dev, away_col = near // BLK, away // COLUMN
    hops = jnp.arange(NY, dtype=jnp.int32)
    asked = (near_dev[None] == ((y + hops) % NY * 2 * NZ + rest)[:, None]) & (away_col == y)[None]
    mine = near_dev == me
    source = mine[None] & (away_col[None] == ((y + hops) % NY)[:, None])
    at_block = mine[None] & ((near % BLK)[None] == jnp.arange(BLK, dtype=jnp.int32)[:, None])
    rank, sums = before(jnp.concatenate([asked, source, at_block], axis=0))
    row = jnp.sum(jnp.where(source, rank[NY:2 * NY] + hops[:, None] * stride_of(cap), 0), axis=0)
    counts = sums[2 * NY:]
    starts = jnp.sum(jnp.where(jnp.arange(BLK)[None, :] < jnp.arange(BLK)[:, None], counts[None, :], 0), axis=1)
    spot = jnp.sum(jnp.where(at_block, rank[2 * NY:] + starts[:, None], 0), axis=0)
    spot = jnp.where(mine, spot, -1)
    sent_at = jnp.sum(jnp.where(asked, rank[:NY] + hops[:, None] * cap + 1, 0), axis=0) - 1
    length = max(far, NY * cap)
    chosen = jnp.stack([sent_at, spot])[:, None, :] == jnp.arange(length, dtype=jnp.int32)[None, :, None]
    value = jnp.stack([away % COLUMN, near % BLK * 1024 + row])
    both = jnp.sum(jnp.where(chosen, value[:, None, :], 0), axis=2)
    count = jnp.sum(counts)
    send_list = both[0]
    tile_list = jnp.where(jnp.arange(length) < count, both[1], (BLK - 1) * 1024)
    last_list = jnp.where(counts > 0, starts + counts - 1, far + jnp.arange(BLK))
    i32 = jnp.int32
    return send_list.astype(i32), tile_list.astype(i32), last_list.astype(i32), count[None].astype(i32)


def excess(near, away, cap, far):
    kinds = jnp.arange(NY + 1, dtype=jnp.int32)
    devices = jnp.arange(2 * NY * NZ, dtype=jnp.int32)
    by_kind = (away // COLUMN == kinds[:, None]) | (kinds == NY)[:, None]
    found = (near // BLK == devices[:, None])[:, None] & by_kind[None]
    counts = jnp.sum(found.astype(jnp.int32), axis=2)
    return jnp.max(jnp.where(kinds == NY, (counts - far) * 1000, counts - cap))


def deliver(*refs):
    copies = [pltpu.make_async_copy(refs[i], refs[4 + i], refs[8].at[i]) for i in range(4)]
    for copy in copies:
        copy.start()
    for copy in copies:
        copy.wait()


def local(queries, keys, values, out_weight, out_grad, pair_list):
    near = jnp.concatenate([pair_list[0], pair_list[1]])
    away = jnp.concatenate([pair_list[1], pair_list[0]])
    arrays = (queries, keys, values, out_weight, out_grad)

    def branch(cap, far, number):
        return lambda: run(cap, far, number, *lists(near, away, cap, far), *arrays)

    over = excess(near, away, 28, 88)
    index = (over > 0).astype(jnp.int32) + (over > 4).astype(jnp.int32)
    results = lax.switch(index, [branch(28, 88, 0), branch(32, 88, 1), branch(64, 160, 2)])
    anywhere = pl.BlockSpec(memory_space=pl.ANY)
    return pl.pallas_call(
        deliver, out_shape=[jax.ShapeDtypeStruct(item.shape, item.dtype) for item in results],
        in_specs=[anywhere] * 4, out_specs=[anywhere] * 4, scratch_shapes=[pltpu.SemaphoreType.DMA((4,))], name="deliver")(*results)


def solution(mesh):
    blocks, weight = P("blk", "hd", None), P("hd", None)
    return jax.shard_map(
        local, mesh=mesh,
        in_specs=(blocks, blocks, blocks, weight, P("blk", None, None), P()),
        out_specs=(blocks,) * 4, check_vma=False)
```
